768 devices in a mesh: gx: 24 (over z_lo, x, core), gy: 32 (over y, z_hi).
Axes of the slice: x: 4, y: 8, z: 12 (z_hi: 4, z_lo: 3; z = z_hi * 3 + z_lo), core: 2. Of those that a mesh axis runs over, the one named last changes fastest.
Arguments:
- precursor: float32 [3, 96, 1024, 128], P(None, 'gx', 'gy'), may hold values from -6 to 6
- u_star: float32 [768, 1024, 128], P('gx', 'gy'), may hold values from -6 to 6
- v_star: float32 [768, 1024, 128], P('gx', 'gy'), may hold values from -6 to 6
- w_star: float32 [768, 1024, 128], P('gx', 'gy'), may hold values from -6 to 6
- heights: int32 [768, 1024], P('gx', 'gy'), may hold values from 0 to 41
Outputs:
- precursor_next: float32 [3, 96, 1024, 128], P(None, 'gx', 'gy')
- pressure: float32 [2, 128, 768, 1024], P(None, 'gy', 'gx')
The draws below stay inside these ranges and needn't reach their ends.
Inputs may be any that keep to these rules, and one draw needn't show every extreme that they name: `heights`: cells of a column at levels below its height are solid.
All inputs are finite; a program needn't handle non-finite values.
Results may differ from the reference program's by a relative error of at most 0.00011.
Values sent between devices are 32-bit elements; how exact they have to be, the bound alone decides.
A program may use at most 32 MiB of HBM per device.

```python
import math
import jax
import jax.numpy as jnp
from jax import lax

NZ = 128
ITERS = 4
NX = 768
NY = 1024
PNX = 96


def set_ends(values, rng, smallest, largest):
    longest = values.shape.index(max(values.shape))
    spots = []
    for shift in (0, 1):
        where = [jax.random.randint(jax.random.fold_in(rng, axis), (), 0, length) for axis, length in enumerate(values.shape)]
        where[longest] = (where[longest] + shift) % values.shape[longest]
        spots.append(tuple(where))
    return values.at[spots[0]].set(smallest).at[spots[1]].set(largest)


def steps_of(key, extent, cuts, low, largest):
    loudness, own = 1.0, jax.random.fold_in(key, 6)
    for dim, blocks in cuts:
        steps = jnp.exp(jax.random.uniform(jax.random.fold_in(own, dim), (blocks,), jnp.float32, low / len(cuts), largest / len(cuts)))
        loudness = loudness * jnp.repeat(steps, extent[dim] // blocks).reshape([-1 if axis == dim else 1 for axis in range(len(extent))])
    return loudness


def gaussian(rng, dims, scale, bound, split=(), dtype=jnp.bfloat16):
    factor_of = steps_of(rng, dims, split, -0.22, 0.18) if split else 1.0
    result = jax.random.normal(rng, dims, jnp.float32) * scale * factor_of
    return jnp.minimum(jnp.maximum(result, -bound), bound).astype(dtype)


def setup_inputs(seed: int = 0) -> dict:
    seeds = jax.random.split(jax.random.key(seed), 6)
    return {
        "precursor": gaussian(seeds[0], (3, PNX, NY, NZ), 1.0, 6.0, ((1, 24), (2, 32)), jnp.float32),
        "u_star": gaussian(seeds[1], (NX, NY, NZ), 1.0, 6.0, ((0, 24), (1, 32)), jnp.float32),
        "v_star": gaussian(seeds[2], (NX, NY, NZ), 1.0, 6.0, ((0, 24), (1, 32)), jnp.float32),
        "w_star": gaussian(seeds[3], (NX, NY, NZ), 1.0, 6.0, ((0, 24), (1, 32)), jnp.float32),
        "heights": set_ends(jax.random.randint(seeds[4], (NX, NY), 0, NZ // 3), jax.random.fold_in(seeds[4], 1), 0, (NZ // 3) - 1).astype(jnp.int32),
    }


step_size = 0.1
viscosity = 0.2
highest = lax.Precision.HIGHEST

def vertical_table(levels):
    modes = lax.broadcasted_iota(jnp.int32, (levels, levels), 0)
    cells = lax.broadcasted_iota(jnp.int32, (levels, levels), 1)
    phase = modes * (2 * cells + 1) % (4 * levels)
    weight = jnp.where(modes == 0, 1.0, 2.0).astype(jnp.float32) / levels
    return jnp.sqrt(weight) * jnp.cos(phase.astype(jnp.float32) * (math.pi / (2 * levels)))

def span_tables(width):
    rows = lax.broadcasted_iota(jnp.int32, (width, width), 0)
    cols = lax.broadcasted_iota(jnp.int32, (width, width), 1)
    angle = (rows * cols % width).astype(jnp.float32) * (2.0 * math.pi / width)
    scale = 1.0 / math.sqrt(width)
    return (jnp.cos(angle) * scale, jnp.sin(angle) * scale)

def precursor_section(padded):
    center = padded[:, 1:-1, 1:-1]
    east = padded[:, 2:, 1:-1]
    west = padded[:, :-2, 1:-1]
    north = padded[:, 1:-1, 2:]
    south = padded[:, 1:-1, :-2]
    lifted = jnp.pad(center, ((0, 0), (0, 0), (0, 0), (1, 1)))
    above = lifted[..., 2:]
    below = lifted[..., :-2]
    advect = center[0:1] * (east - west) * 0.5 + center[1:2] * (north - south) * 0.5 + center[2:3] * (above - below) * 0.5
    spread = east + west + north + south + above + below - 6.0 * center
    return center + step_size * (viscosity * spread - advect)

def sweep(rhs_both, extended, diagonal):
    return (rhs_both + extended[:, :, :-2] + extended[:, :, 2:]) / diagonal

def reference(precursor, u_star, v_star, w_star, heights):
    padded = jnp.pad(precursor, ((0, 0), (1, 1), (1, 1), (0, 0)), mode='wrap')
    precursor_next = precursor_section(padded)
    inflow = precursor_next[0, -1]
    levels = lax.broadcasted_iota(jnp.int32, u_star.shape, 2)
    open_cells = (levels >= heights[:, :, None]).astype(jnp.float32)
    u_open = u_star * open_cells
    v_open = v_star * open_cells
    w_open = w_star * open_cells
    u_prev = jnp.concatenate([inflow[None], u_open[:-1]], 0)
    v_prev = jnp.roll(v_open, 1, axis=1)
    w_prev = jnp.concatenate([jnp.zeros_like(w_open[:, :, :1]), w_open[:, :, :-1]], 2)
    rhs = -(u_open - u_prev + (v_open - v_prev) + (w_open - w_prev))
    table = vertical_table(NZ)
    coeffs = jnp.einsum('mk,xyk->mxy', table, rhs, precision=highest)
    cos_table, sin_table = span_tables(NY)
    flat = coeffs.reshape(-1, NY)
    real_rhs = jnp.dot(flat, cos_table, precision=highest).reshape(coeffs.shape)
    imag_rhs = -jnp.dot(flat, sin_table, precision=highest).reshape(coeffs.shape)
    rhs_both = jnp.stack([real_rhs, imag_rhs])
    modes = lax.broadcasted_iota(jnp.int32, (NZ, 1, 1), 0).astype(jnp.float32)
    waves = lax.broadcasted_iota(jnp.int32, (1, 1, NY), 2).astype(jnp.float32)
    diagonal = 6.0 - 2.0 * jnp.cos(modes * (math.pi / NZ)) - 2.0 * jnp.cos(waves * (2.0 * math.pi / NY))
    pressure = jnp.zeros_like(rhs_both)
    for turn in range(ITERS):
        extended = jnp.pad(pressure, ((0, 0), (0, 0), (1, 1), (0, 0)))
        pressure = sweep(rhs_both, extended, diagonal)
    return (precursor_next, pressure)
```

```python
import math

import jax
import jax.numpy as jnp
import numpy as np
from jax import lax
from jax.experimental import pallas as pl
from jax.experimental.pallas import tpu as pltpu
from jax.sharding import PartitionSpec as P

ITERS = 4
NY = 8
NZ = 4
MESH = pl.DeviceIdType.MESH
F32 = jnp.float32
BF16 = jnp.bfloat16
CHUNKS = ((0, 1, 2, 3, 12, 13, 14, 15), (4, 5, 6, 7, 8, 9, 10, 11))


def split(value):
    high = value.astype(BF16)
    return high, (value - high.astype(F32)).astype(BF16)


def vertical_tables(levels, groups):
    modes = np.arange(levels)[:, None]
    cells = np.arange(levels)[None, :]
    weight = np.where(modes == 0, 1.0, 2.0) / levels
    table = np.sqrt(weight) * np.cos(modes * (2 * cells + 1) % (4 * levels) * (math.pi / (2 * levels)))
    both = np.zeros((levels, 2, 2, levels))
    both[:, 0, 0] = table
    both[:, 1, 1] = table
    return both.reshape(2 * levels, 2 * levels).astype(np.float32)


def span_tables(width):
    half = width // 2
    y = np.arange(width)[:, None]
    cos = np.cos(y * np.arange(half + 1)[None] % width * (2 * math.pi / width))
    sin = np.sin(y * np.arange(1, half)[None] % width * (2 * math.pi / width))
    table = np.concatenate([cos, -sin], 1) / math.sqrt(width)
    cells = width // (NY * NZ)
    table = table.reshape(NY, NZ, cells, width).transpose(1, 0, 2, 3).reshape(NZ, NY * cells, width)
    return table.astype(np.float32)


def inverse_diagonal(levels, width, groups):
    modes = np.arange(levels).reshape(groups, levels // groups, 1, 1)
    half = width // 2
    waves = np.concatenate([np.arange(half + 1), np.arange(1, half)])
    diagonal = 6.0 - 2.0 * np.cos(modes * (math.pi / levels)) - 2.0 * np.cos(waves * (2 * math.pi / width))
    both = np.broadcast_to(1.0 / diagonal, (groups, levels // groups, 2, width))
    return both.reshape(groups, 2 * levels // groups, width).astype(np.float32)


def lane_shift(value, up):
    levels = value.shape[1]
    lane = lax.broadcasted_iota(jnp.int32, value.shape, 1)
    if up:
        return jnp.where(lane == levels - 1, 0.0, pltpu.roll(value, levels - 1, 1))
    return jnp.where(lane == 0, 0.0, pltpu.roll(value, 1, 1))


def row_shift(value, edge, up):
    count = value.shape[0]
    row = lax.broadcasted_iota(jnp.int32, value.shape, 0)
    if up:
        return jnp.where(row == count - 1, edge, pltpu.roll(value, count - 1, 0))
    return jnp.where(row == 0, edge, pltpu.roll(value, 1, 0))


def stencil(q, a, b, c, east, west, north, south):
    above = lane_shift(q, True)
    below = lane_shift(q, False)
    advect = a * (east - west) * 0.5 + b * (north - south) * 0.5 + c * (above - below) * 0.5
    spread = east + west + north + south + above + below - 6.0 * q
    return q + 0.1 * (0.2 * spread - advect)


def kernel(
    prec_hbm, u_hbm, v_hbm, w_hbm, heights_hbm, vert_hbm, span_hbm, inv_hbm,
    next_hbm, press_hbm,
    prec, u, v, w, heights, vert_f32, span_f32, inv, vert, span_hi, span_lo,
    u_out, south_out, north_out, u_in, south_in, north_in, west_in, east_in, corner_in, u_before,
    rhs, rhs_hi, rhs_lo, outgoing, incoming, bands, left_in, right_in, solved, next_v, press_v,
    load_sem, halo_send, halo_recv, send_sem, recv_sem, edge_send, edge_recv, store_sem,
):
    gx, gy = lax.axis_index("gx"), lax.axis_index("gy")
    count_x, count_y = lax.axis_size("gx"), lax.axis_size("gy")
    my_y, my_z = gy // NZ, gy % NZ
    right, left = (gx + 1) % count_x, (gx + count_x - 1) % count_x
    after, before = (gy + 1) % count_y, (gy + count_y - 1) % count_y
    first, last = gx == 0, gx == count_x - 1

    loads = [
        pltpu.make_async_copy(source, target, load_sem.at[i])
        for i, (source, target) in enumerate(
            (
                (heights_hbm, heights),
                (prec_hbm, prec),
                (u_hbm, u),
                (v_hbm, v),
                (w_hbm, w),
                (vert_hbm, vert_f32),
                (inv_hbm.at[gy], inv),
                (span_hbm, span_f32),
            )
        )
    ]
    for load in loads:
        load.start()

    barrier = pltpu.get_barrier_semaphore()

    def greet(other, _):
        @pl.when(other != gy)
        def _():
            pl.semaphore_signal(barrier, inc=1, device_id={"gy": other}, device_id_type=MESH)

        return 0

    lax.fori_loop(0, count_y, greet, 0)
    pl.semaphore_signal(barrier, inc=1, device_id={"gx": right}, device_id_type=MESH)
    pl.semaphore_signal(barrier, inc=1, device_id={"gx": left}, device_id_type=MESH)

    @pl.when(first)
    def _():
        for other in (before, after):
            pl.semaphore_signal(barrier, inc=1, device_id={"gx": left, "gy": other}, device_id_type=MESH)

    rows, levels = u.shape[1], u.shape[2]
    planes = u.shape[0]
    half = planes // 2
    for load in loads[:4]:
        load.wait()
    tall = heights[...].astype(F32).T
    level = lax.broadcasted_iota(jnp.int32, (rows, levels), 1).astype(F32)

    def opened(x):
        return level >= tall[:, x : x + 1]

    u_out[...] = jnp.where(last, prec[0, 2], jnp.where(opened(planes - 1), u[planes - 1], 0.0))
    for x in range(planes):
        south_out[x : x + 1] = jnp.where(opened(x)[rows - 1 :], v[x, rows - 1 : rows], 0.0)
    for c in range(3):
        for x in range(4):
            south_out[planes + 4 * c + x : planes + 4 * c + x + 1] = prec[c, x, rows - 1 : rows]
            north_out[4 * c + x : 4 * c + x + 1] = prec[c, x, 0:1]

    loads[5].wait()
    vert_rows = vert_f32.shape[0]
    vert[:vert_rows], vert[vert_rows:] = split(vert_f32[...])

    pl.semaphore_wait(barrier, count_y + 1 + jnp.where(last, 2, 0))

    def remote(source, target, i, device):
        return pltpu.make_async_remote_copy(
            source, target, halo_send.at[i], halo_recv.at[i], device_id=device, device_id_type=MESH
        )

    halos = [
        remote(south_out, south_in, 0, {"gy": after}),
        remote(u_out, u_in, 1, {"gx": right}),
        remote(prec.at[:, 3], west_in, 2, {"gx": right}),
        remote(north_out, north_in, 3, {"gy": before}),
        remote(prec.at[:, 0], east_in, 4, {"gx": left}),
    ]
    corners = [
        remote(prec.at[0, 3, pl.ds(rows - 8, 8)], corner_in.at[0], 5, {"gx": right, "gy": after}),
        remote(prec.at[0, 3, pl.ds(0, 8)], corner_in.at[1], 6, {"gx": right, "gy": before}),
    ]

    @pl.when(last)
    def _():
        for copy in corners:
            copy.start()

    for copy in halos:
        copy.start()

    loads[4].wait()
    places = {}
    for c, members in enumerate(CHUNKS):
        for i, x in enumerate(members):
            places[x] = (8 * c + i) * rows
    u_prev = None
    zero_row = jnp.zeros((1, levels), F32)
    for x in range(planes):
        is_open = opened(x)
        u_open = jnp.where(is_open, u[x], 0.0)
        v_open = jnp.where(is_open, v[x], 0.0)
        w_open = jnp.where(is_open, w[x], 0.0)
        u_step = u_open if x == 0 else u_open - u_prev
        value = u_step + (v_open - row_shift(v_open, zero_row, False)) + (w_open - lane_shift(w_open, False))
        rhs[pl.ds(places[x % half], rows), pl.ds(x // half * levels, levels)] = -value
        u_prev = u_open

    halos[0].wait_recv()
    halos[1].wait_recv()

    @pl.when(first)
    def _():
        halos[2].wait_recv()
        for copy in corners:
            copy.wait_recv()
        q, west = west_in[0], u_in[...]
        south = row_shift(q, corner_in[0, 7:8], False)
        north = row_shift(q, corner_in[1, 0:1], True)
        u_before[...] = stencil(q, q, west_in[1], west_in[2], prec[0, 0], west, north, south)

    @pl.when(jnp.logical_not(first))
    def _():
        u_before[...] = u_in[...]


    def transform(c):
        row = lax.broadcasted_iota(jnp.int32, (rows, 2 * levels), 0)
        for i, x in enumerate(CHUNKS[c]):
            here = pl.ds((8 * c + i) * rows, rows)
            value = rhs[here]
            edge = jnp.concatenate([south_in[x : x + 1], south_in[half + x : half + x + 1]], 1)
            value = value + jnp.where(row == 0, edge, 0.0)
            if x == 0:
                value = value + jnp.concatenate([u_before[...], jnp.zeros((rows, levels), F32)], 1)
            rhs_hi[here], rhs_lo[here] = split(value)
        cells = pl.ds(8 * c * rows, 8 * rows)
        dims = (((1,), (1,)), ((), ()))
        main = lax.dot_general(vert[...], rhs_hi[cells], dims, preferred_element_type=F32)
        rest = lax.dot_general(vert[:vert_rows], rhs_lo[cells], dims, preferred_element_type=F32)
        outgoing[c] = main[:vert_rows] + main[vert_rows:] + rest

    def block(c, other):
        return pltpu.make_async_remote_copy(
            outgoing.at[c, pl.ds(pl.multiple_of(8 * other, 8), 8)],
            incoming.at[c, my_z, my_y],
            send_sem.at[c, other],
            recv_sem.at[c, gy],
            device_id={"gy": other},
            device_id_type=MESH,
        )

    def send(c, z):
        def one(i, _):
            other = (my_y + i) % NY * NZ + z

            @pl.when(other != gy)
            def _():
                block(c, other).start()

            return 0

        lax.fori_loop(0, NY, one, 0)

    for c in range(2):
        transform(c)
        send(c, 0)
        incoming[c, my_z, my_y] = outgoing[c, pl.ds(pl.multiple_of(8 * gy, 8), 8)]
    for z in range(1, NZ):
        for c in range(2):
            send(c, z)

    @pl.when(jnp.logical_not(first))
    def _():
        halos[2].wait_recv()

    halos[3].wait_recv()
    halos[4].wait_recv()
    for x in range(4):
        a, b, c = prec[0, x], prec[1, x], prec[2, x]
        for k in range(3):
            q = prec[k, x]
            west = west_in[k] if x == 0 else prec[k, x - 1]
            east = east_in[k] if x == 3 else prec[k, x + 1]
            place = 4 * k + x
            south = row_shift(q, south_in[planes + place : planes + place + 1], False)
            north = row_shift(q, north_in[place : place + 1], True)
            next_v[k, x] = stencil(q, a, b, c, east, west, north, south)
    next_store = pltpu.make_async_copy(next_v, next_hbm, store_sem.at[0])
    next_store.start()

    for load in loads[6:]:
        load.wait()

    def split_span(i, _):
        for z in range(NZ):
            here = pl.ds(pl.multiple_of(i * 32, 32), 32)
            span_hi[z, here], span_lo[z, here] = split(span_f32[z, here])
        return 0

    lax.fori_loop(0, span_f32.shape[1] // 32, split_span, 0)

    lane = lax.broadcasted_iota(jnp.int32, (8, 128), 1)
    low_half, even_block = lane < 64, lane // 32 % 2 == 0

    def regrouped(c, z):
        columns = []
        for y0 in (0, 4):
            cells = []
            for x0 in (0, 128):
                s = [incoming[c, z, y0 + i, :, x0 : x0 + 128] for i in range(4)]
                for i in (0, 1):
                    s[i], s[i + 2] = (
                        jnp.where(low_half, s[i], pltpu.roll(s[i + 2], 64, 1)),
                        jnp.where(low_half, pltpu.roll(s[i], 64, 1), s[i + 2]),
                    )
                for i in (0, 2):
                    s[i], s[i + 1] = (
                        jnp.where(even_block, s[i], pltpu.roll(s[i + 1], 32, 1)),
                        jnp.where(even_block, pltpu.roll(s[i], 96, 1), s[i + 1]),
                    )
                cells += s
            columns.append(jnp.concatenate(cells, 0))
        return jnp.concatenate(columns, 1)

    def receive(c, step):
        z = (my_z + step) % NZ

        def one(i, _):
            other = i * NZ + z

            @pl.when(other != gy)
            def _():
                block_in = pltpu.make_async_remote_copy(
                    outgoing.at[c, pl.ds(pl.multiple_of(8 * other, 8), 8)],
                    incoming.at[c, z, i],
                    send_sem.at[c, other],
                    recv_sem.at[c, other],
                    device_id={"gy": other},
                    device_id_type=MESH,
                )
                block_in.wait_recv()

            return 0

        lax.fori_loop(0, NY, one, 0)
        high, low = split(regrouped(c, z))
        count = high.shape[0]
        both = jnp.concatenate([high, low], 0)
        main = jnp.dot(both, span_hi[z], preferred_element_type=F32)
        rest = jnp.dot(high, span_lo[z], preferred_element_type=F32)
        return main[:count] + main[count:] + rest

    width = span_hi.shape[2]

    def place(c, total, add):
        total = total.reshape(8, 8, width)
        pieces = ((3, 0, 4), (15, 4, 8)) if c == 0 else ((7, 0, 8),)
        for at, begin, end in pieces:
            here = pl.ds(at, end - begin)
            bands[here] = bands[here] + total[begin:end] if add else total[begin:end]

    def edge(i, source, target, device):
        return pltpu.make_async_remote_copy(
            source, target, edge_send.at[i], edge_recv.at[i], device_id=device, device_id_type=MESH
        )

    to_right = edge(0, bands.at[pl.ds(16, 3)], left_in, {"gx": right})
    to_left = edge(1, bands.at[pl.ds(3, 3)], right_in, {"gx": left})

    for c in range(2):
        for step in (0, 1, 3, 2):
            place(c, receive(c, step), step != 0)
        if c == 0:

            @pl.when(jnp.logical_not(last))
            def _():
                to_right.start()

            @pl.when(jnp.logical_not(first))
            def _():
                to_left.start()

    @pl.when(jnp.logical_not(first))
    def _():
        to_right.wait_recv()

    @pl.when(first)
    def _():
        left_in[...] = jnp.zeros_like(left_in)

    @pl.when(jnp.logical_not(last))
    def _():
        to_left.wait_recv()

    @pl.when(last)
    def _():
        right_in[...] = jnp.zeros_like(right_in)

    even = lax.broadcasted_iota(jnp.int32, (8, 128), 0) % 2 == 0
    inside_left = jnp.where(jnp.logical_and(even, first), 0.0, 1.0)
    inside_right = jnp.where(jnp.logical_and(jnp.logical_not(even), last), 0.0, 1.0)
    for lane0 in range(0, width, 128):
        lanes = pl.ds(lane0, 128)
        scale = inv[:, lanes]
        left_scale, right_scale = scale * inside_left, scale * inside_right
        b = [None] * 22
        for i in range(3):
            b[i] = jnp.where(even, pltpu.roll(left_in[i, :, lanes], 7, 0), pltpu.roll(bands[16 + i, :, lanes], 1, 0))
            b[19 + i] = jnp.where(even, pltpu.roll(bands[3 + i, :, lanes], 7, 0), pltpu.roll(right_in[i, :, lanes], 1, 0))
        for i in range(3, 19):
            b[i] = bands[i, :, lanes]
        scales = [left_scale] * 3 + [scale] * 16 + [right_scale] * 3
        p = [b[i] * scales[i] for i in range(22)]
        for turn in range(1, ITERS):
            inner = range(turn, 22 - turn)
            new = [None] * 22
            for i in inner:
                new[i] = (b[i] + p[i - 1] + p[i + 1]) * scales[i]
            p = new
        for i in range(16):
            solved[i, :, lanes] = p[3 + i]

    mirror = (128 - lane) % 128
    origin = lane == 0
    pieces = width // 256
    for i in range(16):
        here = pl.ds(i, 8, stride=half)
        parts = [solved[i, :, 128 * k : 128 * k + 128] for k in range(2 * pieces)]
        turned = [jnp.take_along_axis(part, mirror, axis=1) for part in parts]
        for k in range(pieces):
            press_v[0, k, here] = parts[k]
            press_v[0, pieces + k, here] = jnp.where(origin, turned[pieces - k], turned[pieces - k - 1])
            part = parts[pieces + k]
            press_v[1, k, here] = jnp.where(origin, 0.0, part) if k == 0 else part
            beyond = turned[2 * pieces - k] if k else jnp.zeros_like(part)
            press_v[1, pieces + k, here] = -jnp.where(origin, beyond, turned[2 * pieces - k - 1])
    stores = [
        pltpu.make_async_copy(
            press_v.at[part, k],
            press_hbm.at[part, :, pl.ds(128 * k, 128)],
            store_sem.at[1 + 2 * pieces * part + k],
        )
        for part in range(2)
        for k in range(2 * pieces)
    ]
    for store in stores:
        store.start()

    for copy in halos:
        copy.wait_send()

    @pl.when(last)
    def _():
        for copy in corners:
            copy.wait_send()

    @pl.when(jnp.logical_not(last))
    def _():
        to_right.wait_send()

    @pl.when(jnp.logical_not(first))
    def _():
        to_left.wait_send()

    def sent(other, _):
        @pl.when(other != gy)
        def _():
            for c in range(2):
                block(c, other).wait_send()

        return 0

    lax.fori_loop(0, count_y, sent, 0)
    next_store.wait()
    for store in stores:
        store.wait()


def on_device(precursor, u_star, v_star, w_star, heights):
    planes, rows, levels = u_star.shape
    groups = lax.axis_size("gy")
    width = rows * groups
    vert = vertical_tables(levels, groups)
    span = span_tables(width)
    inv = inverse_diagonal(levels, width, groups)
    half = planes // 2
    per = 2 * levels // groups
    any_space = pl.BlockSpec(memory_space=pl.ANY)
    vmem = pltpu.VMEM
    dma = pltpu.SemaphoreType.DMA
    precursor_next, pressure = pl.pallas_call(
        kernel,
        out_shape=(
            jax.ShapeDtypeStruct(precursor.shape, F32),
            jax.ShapeDtypeStruct((2, levels // groups * planes, width), F32),
        ),
        in_specs=[any_space] * 8,
        out_specs=(any_space, any_space),
        scratch_shapes=[
            vmem(precursor.shape, F32),
            vmem(u_star.shape, F32),
            vmem(u_star.shape, F32),
            vmem(u_star.shape, F32),
            vmem(heights.shape, jnp.int32),
            vmem(vert.shape, F32),
            vmem(span.shape, F32),
            vmem((per, width), F32),
            vmem((2 * vert.shape[0], vert.shape[1]), BF16),
            vmem(span.shape, BF16),
            vmem(span.shape, BF16),
            vmem((rows, levels), F32),
            vmem((planes + 16, levels), F32),
            vmem((16, levels), F32),
            vmem((rows, levels), F32),
            vmem((planes + 16, levels), F32),
            vmem((16, levels), F32),
            vmem((3, rows, levels), F32),
            vmem((3, rows, levels), F32),
            vmem((2, 8, levels), F32),
            vmem((rows, levels), F32),
            vmem((half * rows, 2 * levels), F32),
            vmem((half * rows, 2 * levels), BF16),
            vmem((half * rows, 2 * levels), BF16),
            vmem((2, 2 * levels, half * rows // 2), F32),
            vmem((2, NZ, NY, per, half * rows // 2), F32),
            vmem((half + 6, per, width), F32),
            vmem((3, per, width), F32),
            vmem((3, per, width), F32),
            vmem((half, per, width), F32),
            vmem(precursor.shape, F32),
            vmem((2, width // 128, levels // groups * planes, 128), F32),
            dma((8,)),
            dma((7,)),
            dma((7,)),
            dma((2, groups)),
            dma((2, groups)),
            dma((2,)),
            dma((2,)),
            dma((1 + 2 * width // 128,)),
        ],
        compiler_params=pltpu.CompilerParams(
            collective_id=0, has_side_effects=True, vmem_limit_bytes=56 * 2**20
        ),
        name="section",
    )(precursor, u_star, v_star, w_star, heights, vert, span, inv)
    return precursor_next, pressure.reshape(2, levels // groups, planes, width)


def solution(mesh):
    placed = (
        P(None, "gx", "gy", None),
        P("gx", "gy", None),
        P("gx", "gy", None),
        P("gx", "gy", None),
        P("gx", "gy"),
    )
    return jax.shard_map(
        on_device,
        mesh=mesh,
        in_specs=placed,
        out_specs=(P(None, "gx", "gy", None), P(None, "gy", "gx", None)),
        check_vma=False,
    )
```

```python
import functools
import math

import jax
import jax.numpy as jnp
import numpy as np
from jax import lax
from jax.experimental import pallas as pl
from jax.experimental.pallas import tpu as pltpu
from jax.sharding import PartitionSpec as P

ITERS = 4
NY = 8
NZ = 4
MESH = pl.DeviceIdType.MESH
F32 = jnp.float32
BF16 = jnp.bfloat16
CHUNKS = ((0, 1, 2, 3, 12, 13, 14, 15), (4, 5, 6, 7, 8, 9, 10, 11))


def split(value):
    high = value.astype(BF16)
    return high, (value - high.astype(F32)).astype(BF16)


def vertical_tables(levels, groups):
    modes = np.arange(levels)[:, None]
    cells = np.arange(levels)[None, :]
    weight = np.where(modes == 0, 1.0, 2.0) / levels
    table = np.sqrt(weight) * np.cos(modes * (2 * cells + 1) % (4 * levels) * (math.pi / (2 * levels)))
    both = np.zeros((levels, 2, 2, levels))
    both[:, 0, 0] = table
    both[:, 1, 1] = table
    return both.reshape(2 * levels, 2 * levels).astype(np.float32)


def side_table(levels, groups):
    modes = np.arange(levels)[:, None]
    cells = np.arange(levels)[None, :]
    weight = np.where(modes == 0, 1.0, 2.0) / levels
    table = np.sqrt(weight) * np.cos(modes * (2 * cells + 1) % (4 * levels) * (math.pi / (2 * levels)))
    return table.reshape(groups, -1).astype(np.float32)


def span_tables(width):
    half = width // 2
    y = np.arange(width)[:, None]
    cos = np.cos(y * np.arange(half + 1)[None] % width * (2 * math.pi / width))
    sin = np.sin(y * np.arange(1, half)[None] % width * (2 * math.pi / width))
    table = np.concatenate([cos, -sin], 1) / math.sqrt(width)
    cells = width // (NY * NZ)
    after = np.roll(table[::cells], -1, 0).reshape(NY, NZ, width).transpose(1, 0, 2).reshape(NY * NZ, width)
    table = table.reshape(NY, NZ, cells, width).transpose(1, 0, 2, 3).reshape(NZ, NY * cells, width)
    return table.astype(np.float32), after.astype(np.float32)


def inverse_diagonal(levels, width, groups):
    modes = np.arange(levels).reshape(groups, levels // groups, 1, 1)
    half = width // 2
    waves = np.concatenate([np.arange(half + 1), np.arange(1, half)])
    diagonal = 6.0 - 2.0 * np.cos(modes * (math.pi / levels)) - 2.0 * np.cos(waves * (2 * math.pi / width))
    both = np.broadcast_to(1.0 / diagonal, (groups, levels // groups, 2, width))
    return both.reshape(groups, 2 * levels // groups, width).astype(np.float32)


def lane_shift(value, up):
    levels = value.shape[1]
    lane = lax.broadcasted_iota(jnp.int32, value.shape, 1)
    if up:
        return jnp.where(lane == levels - 1, 0.0, pltpu.roll(value, levels - 1, 1))
    return jnp.where(lane == 0, 0.0, pltpu.roll(value, 1, 1))


def row_shift(value, edge, up):
    count = value.shape[0]
    row = lax.broadcasted_iota(jnp.int32, value.shape, 0)
    if up:
        return jnp.where(row == count - 1, edge, pltpu.roll(value, count - 1, 0))
    return jnp.where(row == 0, edge, pltpu.roll(value, 1, 0))


def stencil(q, a, b, c, east, west, north, south):
    above = lane_shift(q, True)
    below = lane_shift(q, False)
    advect = a * (east - west) * 0.5 + b * (north - south) * 0.5 + c * (above - below) * 0.5
    spread = east + west + north + south + above + below - 6.0 * q
    return q + 0.1 * (0.2 * spread - advect)


def three_pass(main, rest, count):
    return main[:count] + main[count:] + rest


def kernel(
    prec_hbm, u_hbm, v_hbm, w_hbm, heights_hbm, vert_hbm, side_hbm, after_hbm, span_hbm,
    next_hbm, bands_hbm, left_hbm, right_hbm, beyond_hbm,
    prec, u, v, w, heights, vert_f32, side_f32, after_f32, span_f32, vert, span_hi, span_lo,
    south_out, north_out, south_in, north_in, west_in, east_in,
    spread, side_out, side_in, side_v, side_u, side_rows,
    rhs, rhs_hi, rhs_lo, outgoing, incoming, bands, beyond, left_out, right_out, left_in, right_in, next_v,
    load_sem, halo_send, halo_recv, side_send, side_recv, send_sem, recv_sem, edge_send, edge_recv, store_sem, late_in, all_in,
):
    gx, gy = lax.axis_index("gx"), lax.axis_index("gy")
    count_x, count_y = lax.axis_size("gx"), lax.axis_size("gy")
    my_y, my_z = gy // NZ, gy % NZ
    right, left = (gx + 1) % count_x, (gx + count_x - 1) % count_x
    after, before = (gy + 1) % count_y, (gy + count_y - 1) % count_y
    first, last = gx == 0, gx == count_x - 1
    early = my_z < 2

    loads = [
        pltpu.make_async_copy(source, target, load_sem.at[i])
        for i, (source, target) in enumerate(
            (
                (prec_hbm, prec),
                (heights_hbm, heights),
                (u_hbm, u),
                (v_hbm, v),
                (w_hbm, w),
                (vert_hbm, vert_f32),
                (side_hbm, side_f32),
                (after_hbm, after_f32),
                (span_hbm, span_f32),
            )
        )
    ]
    for load in loads:
        load.start()

    barrier = pltpu.get_barrier_semaphore()

    def greet_line(sem, zs):
        for z in zs:

            def greet(y, _):
                other = y * NZ + z

                @pl.when(other != gy)
                def _():
                    pl.semaphore_signal(sem, inc=1, device_id={"gy": other}, device_id_type=MESH)

                return 0

            lax.fori_loop(0, NY, greet, 0)

    pl.semaphore_signal(barrier, inc=1, device_id={"gx": right}, device_id_type=MESH)
    pl.semaphore_signal(barrier, inc=1, device_id={"gx": left}, device_id_type=MESH)

    @pl.when(early)
    def _():
        greet_line(barrier, (2, 3, 0, 1))

    @pl.when(my_z == 2)
    def _():
        greet_line(barrier, (3,))
        pl.semaphore_wait(barrier, 2 * NY + 2)
        greet_line(late_in.at[0], (0, 1))

    @pl.when(my_z == 3)
    def _():
        pl.semaphore_wait(barrier, 3 * NY + 2)
        greet_line(late_in.at[1], (0, 1, 2))

    rows, levels = u.shape[1], u.shape[2]
    planes = u.shape[0]
    half = planes // 2
    loads[0].wait()
    for c in range(3):
        for x in range(4):
            south_out[4 * c + x : 4 * c + x + 1] = prec[c, x, rows - 1 : rows]
            north_out[4 * c + x : 4 * c + x + 1] = prec[c, x, 0:1]

    def remote(source, target, i, device):
        return pltpu.make_async_remote_copy(
            source, target, halo_send.at[i], halo_recv.at[i], device_id=device, device_id_type=MESH
        )

    halos = [
        remote(south_out, south_in, 0, {"gy": after}),
        remote(north_out, north_in, 1, {"gy": before}),
        remote(prec.at[:, 3], west_in, 2, {"gx": right}),
        remote(prec.at[:, 0], east_in, 3, {"gx": left}),
    ]

    def send_halos(south, north):
        halos[2].start()
        halos[3].start()

        @pl.when(south)
        def _():
            halos[0].start()

        @pl.when(north)
        def _():
            halos[1].start()

    @pl.when(jnp.logical_not(early))
    def _():
        send_halos(my_z == 3, my_z >= 2)

    spread[...] = jnp.zeros_like(spread)
    for load in loads[1:5]:
        load.wait()
    tall = heights[...].astype(F32).T
    level = lax.broadcasted_iota(jnp.int32, (rows, levels), 1).astype(F32)
    places = {}
    for c, members in enumerate(CHUNKS):
        for i, x in enumerate(members):
            places[x] = (8 * c + i) * rows
    u_prev = None
    zero_row = jnp.zeros((1, levels), F32)
    for x in range(planes):
        is_open = level >= tall[:, x : x + 1]
        u_open = jnp.where(is_open, u[x], 0.0)
        v_open = jnp.where(is_open, v[x], 0.0)
        w_open = jnp.where(is_open, w[x], 0.0)
        u_step = u_open if x == 0 else u_open - u_prev
        value = u_step + (v_open - row_shift(v_open, zero_row, False)) + (w_open - lane_shift(w_open, False))
        rhs[pl.ds(places[x % half], rows), pl.ds(x // half * levels, levels)] = -value
        u_prev = u_open
        for m in range(4):
            at = 8 * (x % half) + 2 * m + x // half
            spread[m, at : at + 1] = v_open[rows - 1 :]

    def side(plane):
        for m in range(4):
            spread[m, 4 * rows + m * rows : 4 * rows + (m + 1) * rows] = plane
        table = side_f32[...]
        count = table.shape[0]
        table_hi, table_lo = split(table)
        value_hi, value_lo = split(jnp.concatenate([spread[m] for m in range(4)], 1))
        dims = (((1,), (1,)), ((), ()))
        main = lax.dot_general(jnp.concatenate([table_hi, table_lo], 0), value_hi, dims, preferred_element_type=F32)
        rest = lax.dot_general(table_hi, value_lo, dims, preferred_element_type=F32)
        value = three_pass(main, rest, count)
        for p in range(count):
            side_out[p, 0:1] = value[p : p + 1, :128]
            side_out[p, 1:2] = value[p : p + 1, 128:]
        side_in[my_z, my_y] = side_out[gy]

    loads[5].wait()
    loads[6].wait()
    vert_rows = vert_f32.shape[0]
    vert[:vert_rows], vert[vert_rows:] = split(vert_f32[...])

    def transform(c):
        for i in range(8):
            here = pl.ds((8 * c + i) * rows, rows)
            rhs_hi[here], rhs_lo[here] = split(rhs[here])
        cells = pl.ds(8 * c * rows, 8 * rows)
        dims = (((1,), (1,)), ((), ()))
        main = lax.dot_general(vert[...], rhs_hi[cells], dims, preferred_element_type=F32)
        rest = lax.dot_general(vert[:vert_rows], rhs_lo[cells], dims, preferred_element_type=F32)
        outgoing[c] = three_pass(main, rest, vert_rows)
        incoming[c, my_z, my_y] = outgoing[c, pl.ds(pl.multiple_of(8 * gy, 8), 8)]

    def block(c, other, z, y):
        return pltpu.make_async_remote_copy(
            outgoing.at[c, pl.ds(pl.multiple_of(8 * other, 8), 8)],
            incoming.at[c, z, y],
            send_sem.at[c, other],
            recv_sem.at[c, z * NY + y],
            device_id={"gy": other},
            device_id_type=MESH,
        )

    def side_block(other, z, y):
        return pltpu.make_async_remote_copy(
            side_out.at[other],
            side_in.at[z, y],
            side_send.at[other],
            side_recv.at[z * NY + y],
            device_id={"gy": other},
            device_id_type=MESH,
        )

    def send(make, z):
        def one(i, _):
            other = (my_y + i) % NY * NZ + z

            @pl.when(other != gy)
            def _():
                make(other, my_z, my_y).start()

            return 0

        lax.fori_loop(0, NY, one, 0)

    def send_side(z):
        @pl.when(jnp.logical_not(last))
        def _():
            send(side_block, z)

    side(u_prev)
    transform(0)

    def split_tables():
        loads[7].wait()
        loads[8].wait()

        def split_span(i, _):
            for z in range(NZ):
                here = pl.ds(pl.multiple_of(i * 32, 32), 32)
                span_hi[z, here], span_lo[z, here] = split(span_f32[z, here])
            return 0

        lax.fori_loop(0, span_f32.shape[1] // 32, split_span, 0)

    @pl.when(early)
    def _():
        split_tables()
        pl.semaphore_wait(barrier, 2 * NY + 1)
        send_halos(my_z == 0, my_z == 1)

    def send_middle(z):
        @pl.when(jnp.logical_not(last))
        def _():
            send(functools.partial(block, 1), z)

    def send_all(z):
        send_side(z)
        send(functools.partial(block, 0), z)
        send_middle(z)

    for z in (0, 1):
        send_side(z)
        send(functools.partial(block, 0), z)
    transform(1)
    for z in (0, 1):
        send_middle(z)

    @pl.when(early)
    def _():
        pl.semaphore_wait(late_in.at[0], NY)

    @pl.when(my_z == 0)
    def _():
        pl.semaphore_signal(all_in, inc=1, device_id={"gy": my_y * NZ + 2}, device_id_type=MESH)

    @pl.when(my_z == 1)
    def _():
        halos[0].start()

    @pl.when(my_z != 2)
    def _():
        send_all(2)

    @pl.when(my_z != 3)
    def _():
        pl.semaphore_wait(late_in.at[1], NY)

    @pl.when(my_z == 0)
    def _():
        pl.semaphore_signal(all_in, inc=1, device_id={"gy": my_y * NZ + 3}, device_id_type=MESH)
        halos[1].start()

    @pl.when(my_z == 2)
    def _():
        halos[0].start()

    @pl.when(my_z != 3)
    def _():
        send_all(3)

    @pl.when(jnp.logical_not(early))
    def _():
        split_tables()

    for copy in halos:
        copy.wait_recv()
    for x in (3, 2, 1, 0):
        a, b, c = prec[0, x], prec[1, x], prec[2, x]
        for k in range(3):
            q = prec[k, x]
            west = west_in[k] if x == 0 else prec[k, x - 1]
            east = east_in[k] if x == 3 else prec[k, x + 1]
            place = 4 * k + x
            south = row_shift(q, south_in[place : place + 1], False)
            north = row_shift(q, north_in[place : place + 1], True)
            next_v[k, x] = stencil(q, a, b, c, east, west, north, south)
    next_store = pltpu.make_async_copy(next_v, next_hbm, store_sem.at[0])
    next_store.start()

    @pl.when(last)
    def _():
        side(next_v[0, 3])
        for z in range(NZ):

            @pl.when(jnp.logical_or(early, my_z != z))
            def _():
                send(side_block, z)

        for z in range(NZ):

            @pl.when(jnp.logical_or(early, my_z != z))
            def _():
                send(functools.partial(block, 1), z)

    for z in (2, 3):

        @pl.when(my_z == z)
        def _():
            pl.semaphore_wait(all_in, 1)
            send(side_block, z)
            for c in range(2):
                send(functools.partial(block, c), z)

    side_u[...] = jnp.zeros_like(side_u)
    side_rows[...] = jnp.zeros_like(side_rows)

    lane = lax.broadcasted_iota(jnp.int32, (8, 128), 1)
    low_half, even_block = lane < 64, lane // 32 % 2 == 0

    def exchanged(s):
        s = list(s)
        for i in (0, 1):
            s[i], s[i + 2] = (
                jnp.where(low_half, s[i], pltpu.roll(s[i + 2], 64, 1)),
                jnp.where(low_half, pltpu.roll(s[i], 64, 1), s[i + 2]),
            )
        for i in (0, 2):
            s[i], s[i + 1] = (
                jnp.where(even_block, s[i], pltpu.roll(s[i + 1], 32, 1)),
                jnp.where(even_block, pltpu.roll(s[i], 96, 1), s[i + 1]),
            )
        return s

    def regrouped(c, z):
        columns = []
        for y0 in (0, 4):
            cells = []
            for x0 in (0, 128):
                cells += exchanged([incoming[c, z, y0 + i, :, x0 : x0 + 128] for i in range(4)])
            columns.append(jnp.concatenate(cells, 0))
        return jnp.concatenate(columns, 1)

    def sides(z):
        for y in range(NY):
            both = side_in[z, y]
            side_v[pl.ds(z * NY + y, 1)] = both[0:1]
            at = 8 * (y % 4) + y // 4
            side_u[at : at + 1] = both[1:2]
        found = exchanged([side_u[8 * i : 8 * i + 8] for i in range(4)])
        for m in range(4):
            for y0 in range(2):
                side_rows[y0, 2 * m + 1 : 2 * m + 2] = found[m][y0 : y0 + 1]
        return jnp.concatenate([side_rows[0], side_rows[1]], 1)

    def arrived(make, z):
        def one(i, _):
            other = i * NZ + z

            @pl.when(other != gy)
            def _():
                make(other, z, i).wait_recv()

            return 0

        lax.fori_loop(0, NY, one, 0)

    def receive(c, step):
        z = step if step < 2 else jnp.where(my_z == 2, 5 - step, step)
        if c == 0:
            arrived(side_block, z)
        arrived(functools.partial(block, c), z)
        value = regrouped(c, z)
        if c == 0:
            value = jnp.concatenate([value, sides(z)], 0)
        high, low = split(value)
        main = jnp.dot(jnp.concatenate([high, low], 0), span_hi[z], preferred_element_type=F32)
        rest = jnp.dot(high, span_lo[z], preferred_element_type=F32)
        return three_pass(main, rest, value.shape[0])

    width = span_hi.shape[2]
    even = lax.broadcasted_iota(jnp.int32, (8, width), 0) % 2 == 0

    def edge(i, source, target, device):
        return pltpu.make_async_remote_copy(
            source, target, edge_send.at[i], edge_recv.at[i], device_id=device, device_id_type=MESH
        )

    to_right = edge(0, left_out, left_in, {"gx": right})
    to_left = edge(1, right_out, right_in, {"gx": left})

    for i, step in enumerate(range(NZ)):
        total = receive(0, step)
        for k, x in enumerate(CHUNKS[0]):
            part = total[8 * k : 8 * k + 8]
            bands[x] = part if i == 0 else bands[x] + part
        part = total[64:72]
        beyond[...] = part if i == 0 else beyond[...] + part
    high, low = split(side_v[...].T)
    after_hi, after_lo = split(after_f32[...])
    count = high.shape[0]
    total = three_pass(
        jnp.dot(jnp.concatenate([high, low], 0), after_hi, preferred_element_type=F32),
        jnp.dot(high, after_lo, preferred_element_type=F32),
        count,
    )
    for x in range(half):
        part = total[8 * x : 8 * x + 8]
        bands[x] = bands[x] + part if x in CHUNKS[0] else part
    left_out[0] = jnp.where(even, pltpu.roll(bands[half - 3], 7, 0), bands[half - 2])
    left_out[1] = jnp.where(even, pltpu.roll(bands[half - 1], 7, 0), beyond[...])
    right_out[0] = jnp.where(even, bands[0], pltpu.roll(bands[1], 1, 0))
    right_out[1] = bands[2]
    to_right.start()

    @pl.when(jnp.logical_not(first))
    def _():
        to_left.start()

    for step in range(NZ):
        total = receive(1, step)
        for k, x in enumerate(CHUNKS[1]):
            bands[x] = bands[x] + total[8 * k : 8 * k + 8]

    stores = [
        pltpu.make_async_copy(bands, bands_hbm, store_sem.at[1]),
        pltpu.make_async_copy(beyond, beyond_hbm, store_sem.at[2]),
        pltpu.make_async_copy(left_in, left_hbm, store_sem.at[3]),
        pltpu.make_async_copy(right_in, right_hbm, store_sem.at[4]),
    ]
    stores[0].start()
    stores[1].start()
    to_right.wait_recv()
    stores[2].start()

    @pl.when(jnp.logical_not(last))
    def _():
        to_left.wait_recv()

    @pl.when(last)
    def _():
        right_in[...] = jnp.zeros_like(right_in)

    stores[3].start()

    for copy in halos:
        copy.wait_send()
    to_right.wait_send()

    @pl.when(jnp.logical_not(first))
    def _():
        to_left.wait_send()

    def sent(other, _):
        @pl.when(other != gy)
        def _():
            side_block(other, my_z, my_y).wait_send()
            for c in range(2):
                block(c, other, my_z, my_y).wait_send()

        return 0

    lax.fori_loop(0, count_y, sent, 0)
    next_store.wait()
    for store in stores:
        store.wait()


def finish(
    next_in, bands_hbm, left_hbm, right_hbm, beyond_hbm, inv_hbm,
    next_hbm, press_hbm,
    bands, left_in, right_in, beyond, inv, next_v, solved, press_v,
    load_sem, store_sem,
):
    gx, gy = lax.axis_index("gx"), lax.axis_index("gy")
    first, last = gx == 0, gx == lax.axis_size("gx") - 1
    width = inv.shape[1]
    half = bands.shape[0]
    loads = [
        pltpu.make_async_copy(source, target, load_sem.at[i])
        for i, (source, target) in enumerate(
            (
                (bands_hbm, bands),
                (left_hbm, left_in),
                (right_hbm, right_in),
                (beyond_hbm, beyond),
                (inv_hbm.at[gy], inv),
                (next_in, next_v),
            )
        )
    ]
    for load in loads:
        load.start()
    for load in loads:
        load.wait()
    next_store = pltpu.make_async_copy(next_v, next_hbm, load_sem.at[6])
    next_store.start()

    lane = lax.broadcasted_iota(jnp.int32, (8, 128), 1)
    even = lax.broadcasted_iota(jnp.int32, (8, 128), 0) % 2 == 0
    inside_left = jnp.where(jnp.logical_and(even, first), 0.0, 1.0)
    inside_right = jnp.where(jnp.logical_and(jnp.logical_not(even), last), 0.0, 1.0)
    mirror = (128 - lane) % 128
    origin = lane == 0
    pieces = width // 256

    def solve(lane0):
        lanes = pl.ds(lane0, 128)
        scale = inv[:, lanes]
        left_scale, right_scale = scale * inside_left, scale * inside_right
        b = [bands[max(i - 3, 0) if i < 19 else 0, :, lanes] for i in range(22)]
        before = [left_in[i, :, lanes] for i in range(2)]
        behind = [right_in[i, :, lanes] for i in range(2)]
        add = beyond[:, lanes]
        before = [before[0], pltpu.roll(before[0], 7, 0), before[1], pltpu.roll(before[1], 7, 0)]
        behind = [pltpu.roll(behind[0], 1, 0) + add, behind[0], pltpu.roll(behind[1], 1, 0)]
        b[3] = jnp.where(even, b[3] + before[3], b[3])
        for i in range(3):
            b[i] = jnp.where(even, before[i], pltpu.roll(b[16 + i], 1, 0))
            b[19 + i] = jnp.where(even, pltpu.roll(bands[i, :, lanes], 7, 0), behind[i])
        scales = [left_scale] * 3 + [scale] * 16 + [right_scale] * 3
        p = [b[i] * scales[i] for i in range(22)]
        for turn in range(1, ITERS):
            new = [None] * 22
            for i in range(turn, 22 - turn):
                new[i] = (b[i] + p[i - 1] + p[i + 1]) * scales[i]
            p = new
        for i in range(half):
            solved[i, :, lanes] = p[3 + i]

    def write(part):
        stores = [
            pltpu.make_async_copy(
                press_v.at[part, k],
                press_hbm.at[part, :, pl.ds(128 * k, 128)],
                store_sem.at[2 * pieces * part + k],
            )
            for k in range(2 * pieces)
        ]
        for store in stores:
            store.start()
        return stores

    for k in range(pieces, 2 * pieces):
        solve(128 * k)
    for i in range(half):
        here = pl.ds(i, 8, stride=half)
        parts = [solved[i, :, 128 * k : 128 * k + 128] for k in range(pieces, 2 * pieces)]
        turned = [jnp.take_along_axis(part, mirror, axis=1) for part in parts]
        for k in range(pieces):
            press_v[1, k, here] = parts[k] if k else jnp.where(origin, 0.0, parts[k])
            beyond_part = turned[pieces - k] if k else jnp.zeros_like(parts[k])
            press_v[1, pieces + k, here] = -jnp.where(origin, beyond_part, turned[pieces - k - 1])
    stores = write(1)
    for k in range(pieces):
        solve(128 * k)
    for i in range(half):
        here = pl.ds(i, 8, stride=half)
        parts = [solved[i, :, 128 * k : 128 * k + 128] for k in range(pieces + 1)]
        turned = [jnp.take_along_axis(part, mirror, axis=1) for part in parts]
        for k in range(pieces):
            press_v[0, k, here] = parts[k]
            press_v[0, pieces + k, here] = jnp.where(origin, turned[pieces - k], turned[pieces - k - 1])
    stores += write(0)
    next_store.wait()
    for store in stores:
        store.wait()


def on_device(precursor, u_star, v_star, w_star, heights):
    planes, rows, levels = u_star.shape
    groups = lax.axis_size("gy")
    width = rows * groups
    vert = vertical_tables(levels, groups)
    side = side_table(levels, groups)
    span, after = span_tables(width)
    inv = inverse_diagonal(levels, width, groups)
    half = planes // 2
    per = 2 * levels // groups
    any_space = pl.BlockSpec(memory_space=pl.ANY)
    vmem = pltpu.VMEM
    dma = pltpu.SemaphoreType.DMA
    between = (
        jax.ShapeDtypeStruct(precursor.shape, F32),
        jax.ShapeDtypeStruct((half, per, width), F32),
        jax.ShapeDtypeStruct((2, per, width), F32),
        jax.ShapeDtypeStruct((2, per, width), F32),
        jax.ShapeDtypeStruct((per, width), F32),
    )
    held = pl.pallas_call(
        kernel,
        out_shape=between,
        in_specs=[any_space] * 9,
        out_specs=(any_space,) * 5,
        scratch_shapes=[
            vmem(precursor.shape, F32),
            vmem(u_star.shape, F32),
            vmem(u_star.shape, F32),
            vmem(u_star.shape, F32),
            vmem(heights.shape, jnp.int32),
            vmem(vert.shape, F32),
            vmem(side.shape, F32),
            vmem(after.shape, F32),
            vmem(span.shape, F32),
            vmem((2 * vert.shape[0], vert.shape[1]), BF16),
            vmem(span.shape, BF16),
            vmem(span.shape, BF16),
            vmem((16, levels), F32),
            vmem((16, levels), F32),
            vmem((16, levels), F32),
            vmem((16, levels), F32),
            vmem((3, rows, levels), F32),
            vmem((3, rows, levels), F32),
            vmem((4, 2 * 128, levels), F32),
            vmem((groups, 2, 128), F32),
            vmem((NZ, NY, 2, 128), F32),
            vmem((groups, 128), F32),
            vmem((32, 128), F32),
            vmem((2, 16, 128), F32),
            vmem((half * rows, 2 * levels), F32),
            vmem((half * rows, 2 * levels), BF16),
            vmem((half * rows, 2 * levels), BF16),
            vmem((2, 2 * levels, half * rows // 2), F32),
            vmem((2, NZ, NY, per, half * rows // 2), F32),
            vmem((half, per, width), F32),
            vmem((per, width), F32),
            vmem((2, per, width), F32),
            vmem((2, per, width), F32),
            vmem((2, per, width), F32),
            vmem((2, per, width), F32),
            vmem(precursor.shape, F32),
            dma((9,)),
            dma((4,)),
            dma((4,)),
            dma((groups,)),
            dma((groups,)),
            dma((2, groups)),
            dma((2, groups)),
            dma((2,)),
            dma((2,)),
            dma((5,)),
            pltpu.SemaphoreType.REGULAR((2,)),
            pltpu.SemaphoreType.REGULAR,
        ],
        compiler_params=pltpu.CompilerParams(
            collective_id=0, has_side_effects=True, vmem_limit_bytes=56 * 2**20
        ),
        name="section",
    )(precursor, u_star, v_star, w_star, heights, vert, side, after, span)
    precursor_next, pressure = pl.pallas_call(
        finish,
        out_shape=(
            jax.ShapeDtypeStruct(precursor.shape, F32),
            jax.ShapeDtypeStruct((2, levels // groups * planes, width), F32),
        ),
        in_specs=[any_space] * 6,
        out_specs=(any_space,) * 2,
        scratch_shapes=[
            vmem((half, per, width), F32),
            vmem((2, per, width), F32),
            vmem((2, per, width), F32),
            vmem((per, width), F32),
            vmem((per, width), F32),
            vmem(precursor.shape, F32),
            vmem((half, per, width), F32),
            vmem((2, width // 128, levels // groups * planes, 128), F32),
            dma((7,)),
            dma((2 * width // 128,)),
        ],
        compiler_params=pltpu.CompilerParams(vmem_limit_bytes=56 * 2**20),
        name="finish",
    )(*held, inv)
    return precursor_next, pressure.reshape(2, levels // groups, planes, width)


def solution(mesh):
    placed = (
        P(None, "gx", "gy", None),
        P("gx", "gy", None),
        P("gx", "gy", None),
        P("gx", "gy", None),
        P("gx", "gy"),
    )
    return jax.shard_map(
        on_device,
        mesh=mesh,
        in_specs=placed,
        out_specs=(P(None, "gx", "gy", None), P(None, "gy", "gx", None)),
        check_vma=False,
    )
```

```python
import functools
import math

import jax
import jax.numpy as jnp
import numpy as np
from jax import lax
from jax.experimental import pallas as pl
from jax.experimental.pallas import tpu as pltpu
from jax.sharding import PartitionSpec as P

ITERS = 4
NY = 8
NZ = 4
MESH = pl.DeviceIdType.MESH
F32 = jnp.float32
BF16 = jnp.bfloat16
CHUNKS = ((0, 1, 2, 3, 12, 13, 14, 15), (4, 5, 6, 7, 8, 9, 10, 11))


def split(value):
    high = value.astype(BF16)
    return high, (value - high.astype(F32)).astype(BF16)


def vertical_tables(levels, groups):
    modes = np.arange(levels)[:, None]
    cells = np.arange(levels)[None, :]
    weight = np.where(modes == 0, 1.0, 2.0) / levels
    table = np.sqrt(weight) * np.cos(modes * (2 * cells + 1) % (4 * levels) * (math.pi / (2 * levels)))
    both = np.zeros((levels, 2, 2, levels))
    both[:, 0, 0] = table
    both[:, 1, 1] = table
    return both.reshape(2 * levels, 2 * levels).astype(np.float32)


def side_table(levels, groups):
    modes = np.arange(levels)[:, None]
    cells = np.arange(levels)[None, :]
    weight = np.where(modes == 0, 1.0, 2.0) / levels
    table = np.sqrt(weight) * np.cos(modes * (2 * cells + 1) % (4 * levels) * (math.pi / (2 * levels)))
    return table.reshape(groups, -1).astype(np.float32)


def span_tables(width):
    half = width // 2
    y = np.arange(width)[:, None]
    cos = np.cos(y * np.arange(half + 1)[None] % width * (2 * math.pi / width))
    sin = np.sin(y * np.arange(1, half)[None] % width * (2 * math.pi / width))
    table = np.concatenate([cos, -sin], 1) / math.sqrt(width)
    cells = width // (NY * NZ)
    after = np.roll(table[::cells], -1, 0).reshape(NY, NZ, width).transpose(1, 0, 2).reshape(NY * NZ, width)
    table = table.reshape(NY, NZ, cells, width).transpose(1, 0, 2, 3).reshape(NZ, NY * cells, width)
    return table.astype(np.float32), after.astype(np.float32)


def inverse_diagonal(levels, width, groups):
    modes = np.arange(levels).reshape(groups, levels // groups, 1, 1)
    half = width // 2
    waves = np.concatenate([np.arange(half + 1), np.arange(1, half)])
    diagonal = 6.0 - 2.0 * np.cos(modes * (math.pi / levels)) - 2.0 * np.cos(waves * (2 * math.pi / width))
    both = np.broadcast_to(1.0 / diagonal, (groups, levels // groups, 2, width))
    return both.reshape(groups, 2 * levels // groups, width).astype(np.float32)


def lane_shift(value, up):
    levels = value.shape[1]
    lane = lax.broadcasted_iota(jnp.int32, value.shape, 1)
    if up:
        return jnp.where(lane == levels - 1, 0.0, pltpu.roll(value, levels - 1, 1))
    return jnp.where(lane == 0, 0.0, pltpu.roll(value, 1, 1))


def row_shift(value, edge, up):
    count = value.shape[0]
    row = lax.broadcasted_iota(jnp.int32, value.shape, 0)
    if up:
        return jnp.where(row == count - 1, edge, pltpu.roll(value, count - 1, 0))
    return jnp.where(row == 0, edge, pltpu.roll(value, 1, 0))


def stencil(q, a, b, c, east, west, north, south):
    above = lane_shift(q, True)
    below = lane_shift(q, False)
    advect = a * (east - west) * 0.5 + b * (north - south) * 0.5 + c * (above - below) * 0.5
    spread = east + west + north + south + above + below - 6.0 * q
    return q + 0.1 * (0.2 * spread - advect)


def three_pass(main, rest, count):
    return main[:count] + main[count:] + rest


def kernel(
    prec_hbm, u_hbm, v_hbm, w_hbm, heights_hbm, vert_hbm, side_hbm, after_hbm, span_hbm,
    next_v, bands, left_to, right_to, beyond,
    prec, u, v, w, heights, vert_f32, side_f32, after_f32, span_f32, vert, span_hi, span_lo,
    south_out, north_out, south_in, north_in, west_in, east_in,
    spread, side_out, side_in, side_v, side_u, side_rows,
    rhs, rhs_hi, rhs_lo, outgoing, incoming, left_out, right_out, left_in, right_in,
    load_sem, halo_send, halo_recv, side_send, side_recv, send_sem, recv_sem, edge_send, edge_recv, late_in, all_in,
):
    gx, gy = lax.axis_index("gx"), lax.axis_index("gy")
    count_x, count_y = lax.axis_size("gx"), lax.axis_size("gy")
    my_y, my_z = gy // NZ, gy % NZ
    right, left = (gx + 1) % count_x, (gx + count_x - 1) % count_x
    after, before = (gy + 1) % count_y, (gy + count_y - 1) % count_y
    first, last = gx == 0, gx == count_x - 1
    early = my_z < 2

    loads = [
        pltpu.make_async_copy(source, target, load_sem.at[i])
        for i, (source, target) in enumerate(
            (
                (prec_hbm, prec),
                (heights_hbm, heights),
                (u_hbm, u),
                (v_hbm, v),
                (w_hbm, w),
                (vert_hbm, vert_f32),
                (side_hbm, side_f32),
                (after_hbm, after_f32),
                (span_hbm, span_f32),
            )
        )
    ]
    for load in loads:
        load.start()

    barrier = pltpu.get_barrier_semaphore()

    def greet_line(sem, zs):
        for z in zs:

            def greet(y, _):
                other = y * NZ + z

                @pl.when(other != gy)
                def _():
                    pl.semaphore_signal(sem, inc=1, device_id={"gy": other}, device_id_type=MESH)

                return 0

            lax.fori_loop(0, NY, greet, 0)

    pl.semaphore_signal(barrier, inc=1, device_id={"gx": right}, device_id_type=MESH)
    pl.semaphore_signal(barrier, inc=1, device_id={"gx": left}, device_id_type=MESH)

    @pl.when(early)
    def _():
        greet_line(barrier, (2, 3, 0, 1))

    @pl.when(my_z == 2)
    def _():
        greet_line(barrier, (3,))
        pl.semaphore_wait(barrier, 2 * NY + 2)
        greet_line(late_in.at[0], (0, 1))

    @pl.when(my_z == 3)
    def _():
        pl.semaphore_wait(barrier, 3 * NY + 2)
        greet_line(late_in.at[1], (0, 1, 2))

    rows, levels = u.shape[1], u.shape[2]
    planes = u.shape[0]
    half = planes // 2
    loads[0].wait()
    for c in range(3):
        for x in range(4):
            south_out[4 * c + x : 4 * c + x + 1] = prec[c, x, rows - 1 : rows]
            north_out[4 * c + x : 4 * c + x + 1] = prec[c, x, 0:1]

    def remote(source, target, i, device):
        return pltpu.make_async_remote_copy(
            source, target, halo_send.at[i], halo_recv.at[i], device_id=device, device_id_type=MESH
        )

    halos = [
        remote(south_out, south_in, 0, {"gy": after}),
        remote(north_out, north_in, 1, {"gy": before}),
        remote(prec.at[:, 3], west_in, 2, {"gx": right}),
        remote(prec.at[:, 0], east_in, 3, {"gx": left}),
    ]

    def send_halos(south, north):
        halos[2].start()
        halos[3].start()

        @pl.when(south)
        def _():
            halos[0].start()

        @pl.when(north)
        def _():
            halos[1].start()

    @pl.when(jnp.logical_not(early))
    def _():
        send_halos(my_z == 3, my_z >= 2)

    spread[...] = jnp.zeros_like(spread)
    for load in loads[1:5]:
        load.wait()
    tall = heights[...].astype(F32).T
    level = lax.broadcasted_iota(jnp.int32, (rows, levels), 1).astype(F32)
    places = {}
    for c, members in enumerate(CHUNKS):
        for i, x in enumerate(members):
            places[x] = (8 * c + i) * rows
    u_prev = None
    zero_row = jnp.zeros((1, levels), F32)
    for x in range(planes):
        is_open = level >= tall[:, x : x + 1]
        u_open = jnp.where(is_open, u[x], 0.0)
        v_open = jnp.where(is_open, v[x], 0.0)
        w_open = jnp.where(is_open, w[x], 0.0)
        u_step = u_open if x == 0 else u_open - u_prev
        value = u_step + (v_open - row_shift(v_open, zero_row, False)) + (w_open - lane_shift(w_open, False))
        rhs[pl.ds(places[x % half], rows), pl.ds(x // half * levels, levels)] = -value
        u_prev = u_open
        for m in range(4):
            at = 8 * (x % half) + 2 * m + x // half
            spread[m, at : at + 1] = v_open[rows - 1 :]

    def side(plane):
        for m in range(4):
            spread[m, 4 * rows + m * rows : 4 * rows + (m + 1) * rows] = plane
        table = side_f32[...]
        count = table.shape[0]
        table_hi, table_lo = split(table)
        value_hi, value_lo = split(jnp.concatenate([spread[m] for m in range(4)], 1))
        dims = (((1,), (1,)), ((), ()))
        main = lax.dot_general(jnp.concatenate([table_hi, table_lo], 0), value_hi, dims, preferred_element_type=F32)
        rest = lax.dot_general(table_hi, value_lo, dims, preferred_element_type=F32)
        value = three_pass(main, rest, count)
        for p in range(count):
            side_out[p, 0:1] = value[p : p + 1, :128]
            side_out[p, 1:2] = value[p : p + 1, 128:]
        side_in[my_z, my_y] = side_out[gy]

    loads[5].wait()
    loads[6].wait()
    vert_rows = vert_f32.shape[0]
    vert[:vert_rows], vert[vert_rows:] = split(vert_f32[...])

    def transform(c):
        for i in range(8):
            here = pl.ds((8 * c + i) * rows, rows)
            rhs_hi[here], rhs_lo[here] = split(rhs[here])
        cells = pl.ds(8 * c * rows, 8 * rows)
        dims = (((1,), (1,)), ((), ()))
        main = lax.dot_general(vert[...], rhs_hi[cells], dims, preferred_element_type=F32)
        rest = lax.dot_general(vert[:vert_rows], rhs_lo[cells], dims, preferred_element_type=F32)
        outgoing[c] = three_pass(main, rest, vert_rows)
        incoming[c, my_z, my_y] = outgoing[c, pl.ds(pl.multiple_of(8 * gy, 8), 8)]

    def block(c, other, z, y):
        return pltpu.make_async_remote_copy(
            outgoing.at[c, pl.ds(pl.multiple_of(8 * other, 8), 8)],
            incoming.at[c, z, y],
            send_sem.at[c],
            recv_sem.at[c, z],
            device_id={"gy": other},
            device_id_type=MESH,
        )

    def side_block(other, z, y):
        return pltpu.make_async_remote_copy(
            side_out.at[other],
            side_in.at[z, y],
            side_send,
            side_recv.at[z],
            device_id={"gy": other},
            device_id_type=MESH,
        )

    def send(make, z):
        def one(i, _):
            other = (my_y + i) % NY * NZ + z

            @pl.when(other != gy)
            def _():
                make(other, my_z, my_y).start()

            return 0

        lax.fori_loop(0, NY, one, 0)

    def send_side(z):
        @pl.when(jnp.logical_not(last))
        def _():
            send(side_block, z)

    side(u_prev)
    transform(0)

    def split_tables():
        loads[7].wait()
        loads[8].wait()

        def split_span(i, _):
            for z in range(NZ):
                here = pl.ds(pl.multiple_of(i * 32, 32), 32)
                span_hi[z, here], span_lo[z, here] = split(span_f32[z, here])
            return 0

        lax.fori_loop(0, span_f32.shape[1] // 32, split_span, 0)

    @pl.when(early)
    def _():
        split_tables()
        pl.semaphore_wait(barrier, 2 * NY + 1)
        send_halos(my_z == 0, my_z == 1)

    def send_middle(z):
        @pl.when(jnp.logical_not(last))
        def _():
            send(functools.partial(block, 1), z)

    def send_all(z):
        send_side(z)
        send(functools.partial(block, 0), z)
        send_middle(z)

    for z in (0, 1):
        send_side(z)
        send(functools.partial(block, 0), z)
    transform(1)
    for z in (0, 1):
        send_middle(z)

    @pl.when(early)
    def _():
        pl.semaphore_wait(late_in.at[0], NY)

    @pl.when(my_z == 0)
    def _():
        pl.semaphore_signal(all_in, inc=1, device_id={"gy": my_y * NZ + 2}, device_id_type=MESH)

    @pl.when(my_z == 1)
    def _():
        halos[0].start()

    @pl.when(my_z != 2)
    def _():
        send_all(2)

    @pl.when(my_z != 3)
    def _():
        pl.semaphore_wait(late_in.at[1], NY)

    @pl.when(my_z == 0)
    def _():
        pl.semaphore_signal(all_in, inc=1, device_id={"gy": my_y * NZ + 3}, device_id_type=MESH)
        halos[1].start()

    @pl.when(my_z == 2)
    def _():
        halos[0].start()

    @pl.when(my_z != 3)
    def _():
        send_all(3)

    @pl.when(jnp.logical_not(early))
    def _():
        split_tables()

    def same_class():
        for z in (2, 3):

            @pl.when(my_z == z)
            def _():
                pl.semaphore_wait(all_in, 1)
                send(side_block, z)
                for c in range(2):
                    send(functools.partial(block, c), z)

    @pl.when(jnp.logical_and(jnp.logical_not(last), jnp.logical_not(early)))
    def _():
        same_class()

    for copy in halos:
        copy.wait_recv()
    def step(k, x):
        q = prec[k, x]
        west = west_in[k] if x == 0 else prec[k, x - 1]
        east = east_in[k] if x == 3 else prec[k, x + 1]
        place = 4 * k + x
        south = row_shift(q, south_in[place : place + 1], False)
        north = row_shift(q, north_in[place : place + 1], True)
        next_v[k, x] = stencil(q, prec[0, x], prec[1, x], prec[2, x], east, west, north, south)

    step(0, 3)

    @pl.when(last)
    def _():
        side(next_v[0, 3])
        for c in range(2):
            for z in range(NZ):

                @pl.when(jnp.logical_or(early, my_z != z))
                def _():
                    send(functools.partial(block, 1) if c else side_block, z)

    @pl.when(jnp.logical_and(last, jnp.logical_not(early)))
    def _():
        same_class()

    for k in range(3):
        for x in range(4):
            if (k, x) != (0, 3):
                step(k, x)
    side_u[...] = jnp.zeros_like(side_u)
    side_rows[...] = jnp.zeros_like(side_rows)

    lane = lax.broadcasted_iota(jnp.int32, (8, 128), 1)
    low_half, even_block = lane < 64, lane // 32 % 2 == 0

    def exchanged(s):
        s = list(s)
        for i in (0, 1):
            s[i], s[i + 2] = (
                jnp.where(low_half, s[i], pltpu.roll(s[i + 2], 64, 1)),
                jnp.where(low_half, pltpu.roll(s[i], 64, 1), s[i + 2]),
            )
        for i in (0, 2):
            s[i], s[i + 1] = (
                jnp.where(even_block, s[i], pltpu.roll(s[i + 1], 32, 1)),
                jnp.where(even_block, pltpu.roll(s[i], 96, 1), s[i + 1]),
            )
        return s

    def regrouped(c, z):
        columns = []
        for y0 in (0, 4):
            cells = []
            for x0 in (0, 128):
                cells += exchanged([incoming[c, z, y0 + i, :, x0 : x0 + 128] for i in range(4)])
            columns.append(jnp.concatenate(cells, 0))
        return jnp.concatenate(columns, 1)

    def sides(z):
        for y in range(NY):
            both = side_in[z, y]
            side_v[pl.ds(z * NY + y, 1)] = both[0:1]
            at = 8 * (y % 4) + y // 4
            side_u[at : at + 1] = both[1:2]
        found = exchanged([side_u[8 * i : 8 * i + 8] for i in range(4)])
        for m in range(4):
            for y0 in range(2):
                side_rows[y0, 2 * m + 1 : 2 * m + 2] = found[m][y0 : y0 + 1]
        return jnp.concatenate([side_rows[0], side_rows[1]], 1)

    def arrived(buffer, sem, z):
        @pl.when(z == my_z)
        def _():
            here = buffer.at[pl.ds(0, NY - 1)]
            pltpu.make_async_copy(here, here, sem).wait()

        @pl.when(z != my_z)
        def _():
            pltpu.make_async_copy(buffer, buffer, sem).wait()

    def receive(c, step):
        z = step if step < 2 else jnp.where(my_z == 2, 5 - step, step)
        if c == 0:
            arrived(side_in.at[z], side_recv.at[z], z)
        arrived(incoming.at[c, z], recv_sem.at[c, z], z)
        value = regrouped(c, z)
        if c == 0:
            value = jnp.concatenate([value, sides(z)], 0)
        high, low = split(value)
        main = jnp.dot(jnp.concatenate([high, low], 0), span_hi[z], preferred_element_type=F32)
        rest = jnp.dot(high, span_lo[z], preferred_element_type=F32)
        return three_pass(main, rest, value.shape[0])

    width = span_hi.shape[2]
    even = lax.broadcasted_iota(jnp.int32, (8, width), 0) % 2 == 0

    def edge(i, source, target, device):
        return pltpu.make_async_remote_copy(
            source, target, edge_send.at[i], edge_recv.at[i], device_id=device, device_id_type=MESH
        )

    to_right = edge(0, left_out, left_in, {"gx": right})
    to_left = edge(1, right_out, right_in, {"gx": left})

    for i, step in enumerate(range(NZ)):
        total = receive(0, step)
        for k, x in enumerate(CHUNKS[0]):
            part = total[8 * k : 8 * k + 8]
            bands[x] = part if i == 0 else bands[x] + part
        part = total[64:72]
        beyond[...] = part if i == 0 else beyond[...] + part
    high, low = split(side_v[...].T)
    after_hi, after_lo = split(after_f32[...])
    count = high.shape[0]
    total = three_pass(
        jnp.dot(jnp.concatenate([high, low], 0), after_hi, preferred_element_type=F32),
        jnp.dot(high, after_lo, preferred_element_type=F32),
        count,
    )
    for x in range(half):
        part = total[8 * x : 8 * x + 8]
        bands[x] = bands[x] + part if x in CHUNKS[0] else part
    left_out[0] = jnp.where(even, pltpu.roll(bands[half - 3], 7, 0), bands[half - 2])
    left_out[1] = jnp.where(even, pltpu.roll(bands[half - 1], 7, 0), beyond[...])
    right_out[0] = jnp.where(even, bands[0], pltpu.roll(bands[1], 1, 0))
    right_out[1] = bands[2]
    to_right.start()

    @pl.when(jnp.logical_not(first))
    def _():
        to_left.start()

    for step in range(NZ):
        total = receive(1, step)
        for k, x in enumerate(CHUNKS[1]):
            bands[x] = bands[x] + total[8 * k : 8 * k + 8]

    to_right.wait_recv()
    left_to[...] = left_in[...]

    @pl.when(jnp.logical_not(last))
    def _():
        to_left.wait_recv()
        right_to[...] = right_in[...]

    @pl.when(last)
    def _():
        right_to[...] = jnp.zeros_like(right_to)

    for copy in halos:
        copy.wait_send()
    to_right.wait_send()

    @pl.when(jnp.logical_not(first))
    def _():
        to_left.wait_send()

    gone = side_out.at[pl.ds(0, count_y - 1)]
    pltpu.make_async_copy(gone, gone, side_send).wait()
    for c in range(2):
        gone = outgoing.at[c, pl.ds(0, 8 * (count_y - 1))]
        pltpu.make_async_copy(gone, gone, send_sem.at[c]).wait()


def finish(
    next_in, bands, left_in, right_in, beyond, inv_hbm,
    next_hbm, press_hbm,
    inv, solved, press_v,
    load_sem, store_sem,
):
    gx, gy = lax.axis_index("gx"), lax.axis_index("gy")
    first, last = gx == 0, gx == lax.axis_size("gx") - 1
    width = inv.shape[1]
    half = bands.shape[0]
    load = pltpu.make_async_copy(inv_hbm.at[gy], inv, load_sem.at[0])
    load.start()
    next_store = pltpu.make_async_copy(next_in, next_hbm, load_sem.at[1])
    next_store.start()
    load.wait()

    lane = lax.broadcasted_iota(jnp.int32, (8, 128), 1)
    even = lax.broadcasted_iota(jnp.int32, (8, 128), 0) % 2 == 0
    inside_left = jnp.where(jnp.logical_and(even, first), 0.0, 1.0)
    inside_right = jnp.where(jnp.logical_and(jnp.logical_not(even), last), 0.0, 1.0)
    mirror = (128 - lane) % 128
    origin = lane == 0
    pieces = width // 256

    def solve(lane0):
        lanes = pl.ds(lane0, 128)
        scale = inv[:, lanes]
        left_scale, right_scale = scale * inside_left, scale * inside_right
        b = [bands[max(i - 3, 0) if i < 19 else 0, :, lanes] for i in range(22)]
        before = [left_in[i, :, lanes] for i in range(2)]
        behind = [right_in[i, :, lanes] for i in range(2)]
        add = beyond[:, lanes]
        before = [before[0], pltpu.roll(before[0], 7, 0), before[1], pltpu.roll(before[1], 7, 0)]
        behind = [pltpu.roll(behind[0], 1, 0) + add, behind[0], pltpu.roll(behind[1], 1, 0)]
        b[3] = jnp.where(even, b[3] + before[3], b[3])
        for i in range(3):
            b[i] = jnp.where(even, before[i], pltpu.roll(b[16 + i], 1, 0))
            b[19 + i] = jnp.where(even, pltpu.roll(bands[i, :, lanes], 7, 0), behind[i])
        scales = [left_scale] * 3 + [scale] * 16 + [right_scale] * 3
        p = [b[i] * scales[i] for i in range(22)]
        for turn in range(1, ITERS):
            new = [None] * 22
            for i in range(turn, 22 - turn):
                new[i] = (b[i] + p[i - 1] + p[i + 1]) * scales[i]
            p = new
        for i in range(half):
            solved[i, :, lanes] = p[3 + i]

    def write(part):
        stores = [
            pltpu.make_async_copy(
                press_v.at[part, k],
                press_hbm.at[part, :, pl.ds(128 * k, 128)],
                store_sem.at[2 * pieces * part + k],
            )
            for k in range(2 * pieces)
        ]
        for store in stores:
            store.start()
        return stores

    for k in range(pieces, 2 * pieces):
        solve(128 * k)
    for i in range(half):
        here = pl.ds(i, 8, stride=half)
        parts = [solved[i, :, 128 * k : 128 * k + 128] for k in range(pieces, 2 * pieces)]
        turned = [jnp.take_along_axis(part, mirror, axis=1) for part in parts]
        for k in range(pieces):
            press_v[1, k, here] = parts[k] if k else jnp.where(origin, 0.0, parts[k])
            beyond_part = turned[pieces - k] if k else jnp.zeros_like(parts[k])
            press_v[1, pieces + k, here] = -jnp.where(origin, beyond_part, turned[pieces - k - 1])
    stores = write(1)
    for k in range(pieces):
        solve(128 * k)
    for i in range(half):
        here = pl.ds(i, 8, stride=half)
        parts = [solved[i, :, 128 * k : 128 * k + 128] for k in range(pieces + 1)]
        turned = [jnp.take_along_axis(part, mirror, axis=1) for part in parts]
        for k in range(pieces):
            press_v[0, k, here] = parts[k]
            press_v[0, pieces + k, here] = jnp.where(origin, turned[pieces - k], turned[pieces - k - 1])
    stores += write(0)
    next_store.wait()
    for store in stores:
        store.wait()


def on_device(precursor, u_star, v_star, w_star, heights):
    planes, rows, levels = u_star.shape
    groups = lax.axis_size("gy")
    width = rows * groups
    vert = vertical_tables(levels, groups)
    side = side_table(levels, groups)
    span, after = span_tables(width)
    inv = inverse_diagonal(levels, width, groups)
    half = planes // 2
    per = 2 * levels // groups
    any_space = pl.BlockSpec(memory_space=pl.ANY)
    vmem = pltpu.VMEM
    dma = pltpu.SemaphoreType.DMA
    between = (
        vmem(precursor.shape, F32),
        vmem((half, per, width), F32),
        vmem((2, per, width), F32),
        vmem((2, per, width), F32),
        vmem((per, width), F32),
    )
    held = pl.pallas_call(
        kernel,
        out_shape=between,
        in_specs=[any_space] * 9,
        out_specs=(pl.BlockSpec(memory_space=pltpu.VMEM),) * 5,
        scratch_shapes=[
            vmem(precursor.shape, F32),
            vmem(u_star.shape, F32),
            vmem(u_star.shape, F32),
            vmem(u_star.shape, F32),
            vmem(heights.shape, jnp.int32),
            vmem(vert.shape, F32),
            vmem(side.shape, F32),
            vmem(after.shape, F32),
            vmem(span.shape, F32),
            vmem((2 * vert.shape[0], vert.shape[1]), BF16),
            vmem(span.shape, BF16),
            vmem(span.shape, BF16),
            vmem((16, levels), F32),
            vmem((16, levels), F32),
            vmem((16, levels), F32),
            vmem((16, levels), F32),
            vmem((3, rows, levels), F32),
            vmem((3, rows, levels), F32),
            vmem((4, 2 * 128, levels), F32),
            vmem((groups, 2, 128), F32),
            vmem((NZ, NY, 2, 128), F32),
            vmem((groups, 128), F32),
            vmem((32, 128), F32),
            vmem((2, 16, 128), F32),
            vmem((half * rows, 2 * levels), F32),
            vmem((half * rows, 2 * levels), BF16),
            vmem((half * rows, 2 * levels), BF16),
            vmem((2, 2 * levels, half * rows // 2), F32),
            vmem((2, NZ, NY, per, half * rows // 2), F32),
            vmem((2, per, width), F32),
            vmem((2, per, width), F32),
            vmem((2, per, width), F32),
            vmem((2, per, width), F32),
            dma((9,)),
            dma((4,)),
            dma((4,)),
            dma,
            dma((NZ,)),
            dma((2,)),
            dma((2, NZ)),
            dma((2,)),
            dma((2,)),
            pltpu.SemaphoreType.REGULAR((2,)),
            pltpu.SemaphoreType.REGULAR,
        ],
        compiler_params=pltpu.CompilerParams(
            collective_id=0, has_side_effects=True, vmem_limit_bytes=56 * 2**20
        ),
        name="section",
    )(precursor, u_star, v_star, w_star, heights, vert, side, after, span)
    precursor_next, pressure = pl.pallas_call(
        finish,
        out_shape=(
            jax.ShapeDtypeStruct(precursor.shape, F32),
            jax.ShapeDtypeStruct((2, levels // groups * planes, width), F32),
        ),
        in_specs=[pl.BlockSpec(memory_space=pltpu.VMEM)] * 5 + [any_space],
        out_specs=(any_space,) * 2,
        scratch_shapes=[
            vmem((per, width), F32),
            vmem((half, per, width), F32),
            vmem((2, width // 128, levels // groups * planes, 128), F32),
            dma((2,)),
            dma((2 * width // 128,)),
        ],
        compiler_params=pltpu.CompilerParams(vmem_limit_bytes=32 * 2**20),
        name="finish",
    )(*(pltpu.with_memory_space_constraint(value, pltpu.VMEM) for value in held), inv)
    return precursor_next, pressure.reshape(2, levels // groups, planes, width)


def solution(mesh):
    placed = (
        P(None, "gx", "gy", None),
        P("gx", "gy", None),
        P("gx", "gy", None),
        P("gx", "gy", None),
        P("gx", "gy"),
    )
    return jax.shard_map(
        on_device,
        mesh=mesh,
        in_specs=placed,
        out_specs=(P(None, "gx", "gy", None), P(None, "gy", "gx", None)),
        check_vma=False,
    )
```

```python
import functools
import math

import jax
import jax.numpy as jnp
import numpy as np
from jax import lax
from jax.experimental import pallas as pl
from jax.experimental.pallas import tpu as pltpu
from jax.sharding import PartitionSpec as P

ITERS = 4
NY = 8
NZ = 4
MESH = pl.DeviceIdType.MESH
F32 = jnp.float32
BF16 = jnp.bfloat16
CHUNKS = ((0, 1, 2, 3, 12, 13, 14, 15), (4, 5, 6, 7, 8, 9, 10, 11))


def split(value):
    high = value.astype(BF16)
    return high, (value - high.astype(F32)).astype(BF16)


def vertical_tables(levels, groups):
    modes = np.arange(levels)[:, None]
    cells = np.arange(levels)[None, :]
    weight = np.where(modes == 0, 1.0, 2.0) / levels
    table = np.sqrt(weight) * np.cos(modes * (2 * cells + 1) % (4 * levels) * (math.pi / (2 * levels)))
    both = np.zeros((levels, 2, 2, levels))
    both[:, 0, 0] = table
    both[:, 1, 1] = table
    return both.reshape(2 * levels, 2 * levels).astype(np.float32)


def side_table(levels, groups):
    modes = np.arange(levels)[:, None]
    cells = np.arange(levels)[None, :]
    weight = np.where(modes == 0, 1.0, 2.0) / levels
    table = np.sqrt(weight) * np.cos(modes * (2 * cells + 1) % (4 * levels) * (math.pi / (2 * levels)))
    return table.reshape(groups, -1).astype(np.float32)


def span_tables(width):
    half = width // 2
    y = np.arange(width)[:, None]
    cos = np.cos(y * np.arange(half + 1)[None] % width * (2 * math.pi / width))
    sin = np.sin(y * np.arange(1, half)[None] % width * (2 * math.pi / width))
    table = np.concatenate([cos, -sin], 1) / math.sqrt(width)
    cells = width // (NY * NZ)
    after = np.roll(table[::cells], -1, 0).reshape(NY, NZ, width).transpose(1, 0, 2).reshape(NY * NZ, width)
    table = table.reshape(NY, NZ, cells, width).transpose(1, 0, 2, 3).reshape(NZ, NY * cells, width)
    return table.astype(np.float32), after.astype(np.float32)


def inverse_diagonal(levels, width, groups):
    modes = np.arange(levels).reshape(groups, levels // groups, 1, 1)
    half = width // 2
    waves = np.concatenate([np.arange(half + 1), np.arange(1, half)])
    diagonal = 6.0 - 2.0 * np.cos(modes * (math.pi / levels)) - 2.0 * np.cos(waves * (2 * math.pi / width))
    both = np.broadcast_to(1.0 / diagonal, (groups, levels // groups, 2, width))
    return both.reshape(groups, 2 * levels // groups, width).astype(np.float32)


def lane_shift(value, up):
    levels = value.shape[1]
    lane = lax.broadcasted_iota(jnp.int32, value.shape, 1)
    if up:
        return jnp.where(lane == levels - 1, 0.0, pltpu.roll(value, levels - 1, 1))
    return jnp.where(lane == 0, 0.0, pltpu.roll(value, 1, 1))


def row_shift(value, edge, up):
    count = value.shape[0]
    row = lax.broadcasted_iota(jnp.int32, value.shape, 0)
    if up:
        return jnp.where(row == count - 1, edge, pltpu.roll(value, count - 1, 0))
    return jnp.where(row == 0, edge, pltpu.roll(value, 1, 0))


def stencil(q, a, b, c, east, west, north, south):
    above = lane_shift(q, True)
    below = lane_shift(q, False)
    advect = a * (east - west) * 0.5 + b * (north - south) * 0.5 + c * (above - below) * 0.5
    spread = east + west + north + south + above + below - 6.0 * q
    return q + 0.1 * (0.2 * spread - advect)


def three_pass(main, rest, count):
    return main[:count] + main[count:] + rest


def kernel(
    prec_hbm, u_hbm, v_hbm, w_hbm, heights_hbm, vert_hbm, side_hbm, after_hbm, span_hbm,
    next_v, bands, left_to, right_to, beyond,
    prec, u, v, w, heights, vert_f32, side_f32, after_f32, span_f32, vert, span_hi, span_lo,
    south_out, north_out, south_in, north_in, west_in, east_in,
    spread, side_out, side_in, side_v, side_u, side_rows,
    rhs, rhs_hi, rhs_lo, outgoing, incoming, left_out, right_out, left_in, right_in,
    load_sem, halo_send, halo_recv, side_send, side_recv, send_sem, recv_sem, edge_send, edge_recv, late_in, all_in,
):
    gx, gy = lax.axis_index("gx"), lax.axis_index("gy")
    count_x, count_y = lax.axis_size("gx"), lax.axis_size("gy")
    my_y, my_z = gy // NZ, gy % NZ
    right, left = (gx + 1) % count_x, (gx + count_x - 1) % count_x
    after, before = (gy + 1) % count_y, (gy + count_y - 1) % count_y
    first, last = gx == 0, gx == count_x - 1
    early = my_z < 2

    loads = [
        pltpu.make_async_copy(source, target, load_sem.at[i])
        for i, (source, target) in enumerate(
            (
                (prec_hbm, prec),
                (heights_hbm, heights),
                (u_hbm, u),
                (v_hbm, v),
                (w_hbm, w),
                (vert_hbm, vert_f32),
                (side_hbm, side_f32),
                (after_hbm, after_f32),
                (span_hbm, span_f32),
            )
        )
    ]
    for load in loads:
        load.start()

    barrier = pltpu.get_barrier_semaphore()

    def greet_line(sem, zs):
        for z in zs:

            def greet(y, _):
                other = y * NZ + z

                @pl.when(other != gy)
                def _():
                    pl.semaphore_signal(sem, inc=1, device_id={"gy": other}, device_id_type=MESH)

                return 0

            lax.fori_loop(0, NY, greet, 0)

    pl.semaphore_signal(barrier, inc=1, device_id={"gx": right}, device_id_type=MESH)
    pl.semaphore_signal(barrier, inc=1, device_id={"gx": left}, device_id_type=MESH)

    @pl.when(early)
    def _():
        greet_line(barrier, (2, 3, 0, 1))

    @pl.when(my_z == 2)
    def _():
        greet_line(barrier, (3,))
        pl.semaphore_wait(barrier, 2 * NY + 2)
        greet_line(late_in.at[0], (0, 1))

    @pl.when(my_z == 3)
    def _():
        pl.semaphore_wait(barrier, 3 * NY + 2)
        greet_line(late_in.at[1], (0, 1, 2))

    rows, levels = u.shape[1], u.shape[2]
    planes = u.shape[0]
    half = planes // 2
    loads[0].wait()
    for c in range(3):
        for x in range(4):
            south_out[4 * c + x : 4 * c + x + 1] = prec[c, x, rows - 1 : rows]
            north_out[4 * c + x : 4 * c + x + 1] = prec[c, x, 0:1]

    def remote(source, target, i, device):
        return pltpu.make_async_remote_copy(
            source, target, halo_send.at[i], halo_recv.at[i], device_id=device, device_id_type=MESH
        )

    halos = [
        remote(south_out, south_in, 0, {"gy": after}),
        remote(north_out, north_in, 1, {"gy": before}),
        remote(prec.at[:, 3], west_in, 2, {"gx": right}),
        remote(prec.at[:, 0], east_in, 3, {"gx": left}),
    ]

    def send_halos(south, north):
        halos[2].start()
        halos[3].start()

        @pl.when(south)
        def _():
            halos[0].start()

        @pl.when(north)
        def _():
            halos[1].start()

    @pl.when(jnp.logical_not(early))
    def _():
        send_halos(my_z == 3, my_z >= 2)

    spread[...] = jnp.zeros_like(spread)
    for load in loads[1:5]:
        load.wait()
    tall = heights[...].astype(F32).T
    level = lax.broadcasted_iota(jnp.int32, (rows, levels), 1).astype(F32)
    places = {}
    for c, members in enumerate(CHUNKS):
        for i, x in enumerate(members):
            places[x] = (8 * c + i) * rows
    u_prev = None
    zero_row = jnp.zeros((1, levels), F32)
    for x in range(planes):
        is_open = level >= tall[:, x : x + 1]
        u_open = jnp.where(is_open, u[x], 0.0)
        v_open = jnp.where(is_open, v[x], 0.0)
        w_open = jnp.where(is_open, w[x], 0.0)
        u_step = u_open if x == 0 else u_open - u_prev
        value = u_step + (v_open - row_shift(v_open, zero_row, False)) + (w_open - lane_shift(w_open, False))
        rhs[pl.ds(places[x % half], rows), pl.ds(x // half * levels, levels)] = -value
        u_prev = u_open
        for m in range(4):
            at = 8 * (x % half) + 2 * m + x // half
            spread[m, at : at + 1] = v_open[rows - 1 :]

    def side(plane):
        for m in range(4):
            spread[m, 4 * rows + m * rows : 4 * rows + (m + 1) * rows] = plane
        table = side_f32[...]
        count = table.shape[0]
        table_hi, table_lo = split(table)
        value_hi, value_lo = split(jnp.concatenate([spread[m] for m in range(4)], 1))
        dims = (((1,), (1,)), ((), ()))
        main = lax.dot_general(jnp.concatenate([table_hi, table_lo], 0), value_hi, dims, preferred_element_type=F32)
        rest = lax.dot_general(table_hi, value_lo, dims, preferred_element_type=F32)
        value = three_pass(main, rest, count)
        for p in range(count):
            side_out[p, 0:1] = value[p : p + 1, :128]
            side_out[p, 1:2] = value[p : p + 1, 128:]
        side_in[my_z, my_y] = side_out[gy]

    loads[5].wait()
    loads[6].wait()
    vert_rows = vert_f32.shape[0]
    vert[:vert_rows], vert[vert_rows:] = split(vert_f32[...])

    def transform(c):
        for i in range(8):
            here = pl.ds((8 * c + i) * rows, rows)
            rhs_hi[here], rhs_lo[here] = split(rhs[here])
        cells = pl.ds(8 * c * rows, 8 * rows)
        dims = (((1,), (1,)), ((), ()))
        main = lax.dot_general(vert[...], rhs_hi[cells], dims, preferred_element_type=F32)
        rest = lax.dot_general(vert[:vert_rows], rhs_lo[cells], dims, preferred_element_type=F32)
        outgoing[c] = three_pass(main, rest, vert_rows)
        incoming[c, my_z, my_y] = outgoing[c, pl.ds(pl.multiple_of(8 * gy, 8), 8)]

    def block(c, other, z, y):
        return pltpu.make_async_remote_copy(
            outgoing.at[c, pl.ds(pl.multiple_of(8 * other, 8), 8)],
            incoming.at[c, z, y],
            send_sem.at[c],
            recv_sem.at[c, z],
            device_id={"gy": other},
            device_id_type=MESH,
        )

    def side_block(other, z, y):
        return pltpu.make_async_remote_copy(
            side_out.at[other],
            side_in.at[z, y],
            side_send,
            side_recv.at[z],
            device_id={"gy": other},
            device_id_type=MESH,
        )

    def send(make, z):
        def one(i, _):
            other = (my_y + i) % NY * NZ + z

            @pl.when(other != gy)
            def _():
                make(other, my_z, my_y).start()

            return 0

        lax.fori_loop(0, NY, one, 0)

    def send_side(z):
        @pl.when(jnp.logical_not(last))
        def _():
            send(side_block, z)

    side(u_prev)
    transform(0)

    def split_tables():
        loads[7].wait()
        loads[8].wait()

        def split_span(i, _):
            for z in range(NZ):
                here = pl.ds(pl.multiple_of(i * 32, 32), 32)
                span_hi[z, here], span_lo[z, here] = split(span_f32[z, here])
            return 0

        lax.fori_loop(0, span_f32.shape[1] // 32, split_span, 0)

    @pl.when(early)
    def _():
        split_tables()
        pl.semaphore_wait(barrier, 2 * NY + 1)
        send_halos(my_z == 0, my_z == 1)

    def send_middle(z):
        @pl.when(jnp.logical_not(last))
        def _():
            send(functools.partial(block, 1), z)

    def send_all(z):
        send_side(z)
        send(functools.partial(block, 0), z)
        send_middle(z)

    for z in (0, 1):
        send_side(z)
        send(functools.partial(block, 0), z)
    transform(1)
    for z in (0, 1):
        send_middle(z)

    @pl.when(early)
    def _():
        pl.semaphore_wait(late_in.at[0], NY)

    @pl.when(my_z == 0)
    def _():
        pl.semaphore_signal(all_in, inc=1, device_id={"gy": my_y * NZ + 2}, device_id_type=MESH)

    @pl.when(my_z == 1)
    def _():
        halos[0].start()

    @pl.when(my_z != 2)
    def _():
        send_all(2)

    @pl.when(my_z != 3)
    def _():
        pl.semaphore_wait(late_in.at[1], NY)

    @pl.when(my_z == 0)
    def _():
        pl.semaphore_signal(all_in, inc=1, device_id={"gy": my_y * NZ + 3}, device_id_type=MESH)
        halos[1].start()

    @pl.when(my_z == 2)
    def _():
        halos[0].start()

    @pl.when(my_z != 3)
    def _():
        send_side(3)
        send(functools.partial(block, 0), 3)

    @pl.when(my_z == 2)
    def _():
        send_middle(3)

    @pl.when(jnp.logical_not(early))
    def _():
        split_tables()

    def same_class():
        for z in (2, 3):

            @pl.when(my_z == z)
            def _():
                pl.semaphore_wait(all_in, 1)
                send(side_block, z)
                for c in range(2):
                    send(functools.partial(block, c), z)

    @pl.when(jnp.logical_and(jnp.logical_not(last), jnp.logical_not(early)))
    def _():
        same_class()

    for copy in halos:
        copy.wait_recv()
    def step(k, x):
        q = prec[k, x]
        west = west_in[k] if x == 0 else prec[k, x - 1]
        east = east_in[k] if x == 3 else prec[k, x + 1]
        place = 4 * k + x
        south = row_shift(q, south_in[place : place + 1], False)
        north = row_shift(q, north_in[place : place + 1], True)
        next_v[k, x] = stencil(q, prec[0, x], prec[1, x], prec[2, x], east, west, north, south)

    step(0, 3)

    @pl.when(last)
    def _():
        side(next_v[0, 3])
        for c in range(2):
            for z in range(NZ):

                @pl.when(jnp.logical_and(jnp.logical_or(early, my_z != z), jnp.logical_not(early) if c * z == 3 else True))
                def _():
                    send(functools.partial(block, 1) if c else side_block, z)

    @pl.when(jnp.logical_and(last, jnp.logical_not(early)))
    def _():
        same_class()

    for k in range(3):
        for x in range(4):
            if (k, x) != (0, 3):
                step(k, x)
    side_u[...] = jnp.zeros_like(side_u)
    side_rows[...] = jnp.zeros_like(side_rows)

    lane = lax.broadcasted_iota(jnp.int32, (8, 128), 1)
    low_half, even_block = lane < 64, lane // 32 % 2 == 0

    def exchanged(s):
        s = list(s)
        for i in (0, 1):
            s[i], s[i + 2] = (
                jnp.where(low_half, s[i], pltpu.roll(s[i + 2], 64, 1)),
                jnp.where(low_half, pltpu.roll(s[i], 64, 1), s[i + 2]),
            )
        for i in (0, 2):
            s[i], s[i + 1] = (
                jnp.where(even_block, s[i], pltpu.roll(s[i + 1], 32, 1)),
                jnp.where(even_block, pltpu.roll(s[i], 96, 1), s[i + 1]),
            )
        return s

    def regrouped(c, z):
        columns = []
        for y0 in (0, 4):
            cells = []
            for x0 in (0, 128):
                cells += exchanged([incoming[c, z, y0 + i, :, x0 : x0 + 128] for i in range(4)])
            columns.append(jnp.concatenate(cells, 0))
        return jnp.concatenate(columns, 1)

    def sides(z):
        for y in range(NY):
            both = side_in[z, y]
            side_v[pl.ds(z * NY + y, 1)] = both[0:1]
            at = 8 * (y % 4) + y // 4
            side_u[at : at + 1] = both[1:2]
        found = exchanged([side_u[8 * i : 8 * i + 8] for i in range(4)])
        for m in range(4):
            for y0 in range(2):
                side_rows[y0, 2 * m + 1 : 2 * m + 2] = found[m][y0 : y0 + 1]
        return jnp.concatenate([side_rows[0], side_rows[1]], 1)

    def arrived(buffer, sem, z):
        @pl.when(z == my_z)
        def _():
            here = buffer.at[pl.ds(0, NY - 1)]
            pltpu.make_async_copy(here, here, sem).wait()

        @pl.when(z != my_z)
        def _():
            pltpu.make_async_copy(buffer, buffer, sem).wait()

    def receive(c, step):
        z = step if step < 2 else jnp.where(my_z == 2, 5 - step, step)
        if c == 0:
            arrived(side_in.at[z], side_recv.at[z], z)
        arrived(incoming.at[c, z], recv_sem.at[c, z], z)
        value = regrouped(c, z)
        if c == 0:
            value = jnp.concatenate([value, sides(z)], 0)
        high, low = split(value)
        main = jnp.dot(jnp.concatenate([high, low], 0), span_hi[z], preferred_element_type=F32)
        rest = jnp.dot(high, span_lo[z], preferred_element_type=F32)
        return three_pass(main, rest, value.shape[0])

    width = span_hi.shape[2]
    even = lax.broadcasted_iota(jnp.int32, (8, width), 0) % 2 == 0

    def edge(i, source, target, device):
        return pltpu.make_async_remote_copy(
            source, target, edge_send.at[i], edge_recv.at[i], device_id=device, device_id_type=MESH
        )

    to_right = edge(0, left_out, left_in, {"gx": right})
    to_left = edge(1, right_out, right_in, {"gx": left})

    for i, step in enumerate(range(NZ)):
        total = receive(0, step)
        for k, x in enumerate(CHUNKS[0]):
            part = total[8 * k : 8 * k + 8]
            bands[x] = part if i == 0 else bands[x] + part
        part = total[64:72]
        beyond[...] = part if i == 0 else beyond[...] + part
    high, low = split(side_v[...].T)
    after_hi, after_lo = split(after_f32[...])
    count = high.shape[0]
    total = three_pass(
        jnp.dot(jnp.concatenate([high, low], 0), after_hi, preferred_element_type=F32),
        jnp.dot(high, after_lo, preferred_element_type=F32),
        count,
    )
    for x in range(half):
        part = total[8 * x : 8 * x + 8]
        bands[x] = bands[x] + part if x in CHUNKS[0] else part
    left_out[0] = jnp.where(even, pltpu.roll(bands[half - 3], 7, 0), bands[half - 2])
    left_out[1] = jnp.where(even, pltpu.roll(bands[half - 1], 7, 0), beyond[...])
    right_out[0] = jnp.where(even, bands[0], pltpu.roll(bands[1], 1, 0))
    right_out[1] = bands[2]
    to_right.start()

    @pl.when(jnp.logical_not(first))
    def _():
        to_left.start()

    @pl.when(early)
    def _():
        send(functools.partial(block, 1), 3)

    for step in range(NZ):
        total = receive(1, step)
        for k, x in enumerate(CHUNKS[1]):
            bands[x] = bands[x] + total[8 * k : 8 * k + 8]

    to_right.wait_recv()
    left_to[...] = left_in[...]

    @pl.when(jnp.logical_not(last))
    def _():
        to_left.wait_recv()
        right_to[...] = right_in[...]

    @pl.when(last)
    def _():
        right_to[...] = jnp.zeros_like(right_to)

    for copy in halos:
        copy.wait_send()
    to_right.wait_send()

    @pl.when(jnp.logical_not(first))
    def _():
        to_left.wait_send()

    gone = side_out.at[pl.ds(0, count_y - 1)]
    pltpu.make_async_copy(gone, gone, side_send).wait()
    for c in range(2):
        gone = outgoing.at[c, pl.ds(0, 8 * (count_y - 1))]
        pltpu.make_async_copy(gone, gone, send_sem.at[c]).wait()


def finish(
    next_in, bands, left_in, right_in, beyond, inv_hbm,
    next_hbm, press_hbm,
    inv, solved, press_v,
    load_sem, store_sem,
):
    gx, gy = lax.axis_index("gx"), lax.axis_index("gy")
    first, last = gx == 0, gx == lax.axis_size("gx") - 1
    width = inv.shape[1]
    half = bands.shape[0]
    load = pltpu.make_async_copy(inv_hbm.at[gy], inv, load_sem.at[0])
    load.start()
    next_store = pltpu.make_async_copy(next_in, next_hbm, load_sem.at[1])
    next_store.start()
    load.wait()

    lane = lax.broadcasted_iota(jnp.int32, (8, 128), 1)
    even = lax.broadcasted_iota(jnp.int32, (8, 128), 0) % 2 == 0
    inside_left = jnp.where(jnp.logical_and(even, first), 0.0, 1.0)
    inside_right = jnp.where(jnp.logical_and(jnp.logical_not(even), last), 0.0, 1.0)
    mirror = (128 - lane) % 128
    origin = lane == 0
    pieces = width // 256

    def solve(lane0):
        lanes = pl.ds(lane0, 128)
        scale = inv[:, lanes]
        left_scale, right_scale = scale * inside_left, scale * inside_right
        b = [bands[max(i - 3, 0) if i < 19 else 0, :, lanes] for i in range(22)]
        before = [left_in[i, :, lanes] for i in range(2)]
        behind = [right_in[i, :, lanes] for i in range(2)]
        add = beyond[:, lanes]
        before = [before[0], pltpu.roll(before[0], 7, 0), before[1], pltpu.roll(before[1], 7, 0)]
        behind = [pltpu.roll(behind[0], 1, 0) + add, behind[0], pltpu.roll(behind[1], 1, 0)]
        b[3] = jnp.where(even, b[3] + before[3], b[3])
        for i in range(3):
            b[i] = jnp.where(even, before[i], pltpu.roll(b[16 + i], 1, 0))
            b[19 + i] = jnp.where(even, pltpu.roll(bands[i, :, lanes], 7, 0), behind[i])
        scales = [left_scale] * 3 + [scale] * 16 + [right_scale] * 3
        p = [b[i] * scales[i] for i in range(22)]
        for turn in range(1, ITERS):
            new = [None] * 22
            for i in range(turn, 22 - turn):
                new[i] = (b[i] + p[i - 1] + p[i + 1]) * scales[i]
            p = new
        for i in range(half):
            solved[i, :, lanes] = p[3 + i]

    def write(part):
        stores = [
            pltpu.make_async_copy(
                press_v.at[part, k],
                press_hbm.at[part, :, pl.ds(128 * k, 128)],
                store_sem.at[2 * pieces * part + k],
            )
            for k in range(2 * pieces)
        ]
        for store in stores:
            store.start()
        return stores

    for k in range(pieces, 2 * pieces):
        solve(128 * k)
    for i in range(half):
        here = pl.ds(i, 8, stride=half)
        parts = [solved[i, :, 128 * k : 128 * k + 128] for k in range(pieces, 2 * pieces)]
        turned = [jnp.take_along_axis(part, mirror, axis=1) for part in parts]
        for k in range(pieces):
            press_v[1, k, here] = parts[k] if k else jnp.where(origin, 0.0, parts[k])
            beyond_part = turned[pieces - k] if k else jnp.zeros_like(parts[k])
            press_v[1, pieces + k, here] = -jnp.where(origin, beyond_part, turned[pieces - k - 1])
    stores = write(1)
    for k in range(pieces):
        solve(128 * k)
    for i in range(half):
        here = pl.ds(i, 8, stride=half)
        parts = [solved[i, :, 128 * k : 128 * k + 128] for k in range(pieces + 1)]
        turned = [jnp.take_along_axis(part, mirror, axis=1) for part in parts]
        for k in range(pieces):
            press_v[0, k, here] = parts[k]
            press_v[0, pieces + k, here] = jnp.where(origin, turned[pieces - k], turned[pieces - k - 1])
    stores += write(0)
    next_store.wait()
    for store in stores:
        store.wait()


def on_device(precursor, u_star, v_star, w_star, heights):
    planes, rows, levels = u_star.shape
    groups = lax.axis_size("gy")
    width = rows * groups
    vert = vertical_tables(levels, groups)
    side = side_table(levels, groups)
    span, after = span_tables(width)
    inv = inverse_diagonal(levels, width, groups)
    half = planes // 2
    per = 2 * levels // groups
    any_space = pl.BlockSpec(memory_space=pl.ANY)
    vmem = pltpu.VMEM
    dma = pltpu.SemaphoreType.DMA
    between = (
        vmem(precursor.shape, F32),
        vmem((half, per, width), F32),
        vmem((2, per, width), F32),
        vmem((2, per, width), F32),
        vmem((per, width), F32),
    )
    held = pl.pallas_call(
        kernel,
        out_shape=between,
        in_specs=[any_space] * 9,
        out_specs=(pl.BlockSpec(memory_space=pltpu.VMEM),) * 5,
        scratch_shapes=[
            vmem(precursor.shape, F32),
            vmem(u_star.shape, F32),
            vmem(u_star.shape, F32),
            vmem(u_star.shape, F32),
            vmem(heights.shape, jnp.int32),
            vmem(vert.shape, F32),
            vmem(side.shape, F32),
            vmem(after.shape, F32),
            vmem(span.shape, F32),
            vmem((2 * vert.shape[0], vert.shape[1]), BF16),
            vmem(span.shape, BF16),
            vmem(span.shape, BF16),
            vmem((16, levels), F32),
            vmem((16, levels), F32),
            vmem((16, levels), F32),
            vmem((16, levels), F32),
            vmem((3, rows, levels), F32),
            vmem((3, rows, levels), F32),
            vmem((4, 2 * 128, levels), F32),
            vmem((groups, 2, 128), F32),
            vmem((NZ, NY, 2, 128), F32),
            vmem((groups, 128), F32),
            vmem((32, 128), F32),
            vmem((2, 16, 128), F32),
            vmem((half * rows, 2 * levels), F32),
            vmem((half * rows, 2 * levels), BF16),
            vmem((half * rows, 2 * levels), BF16),
            vmem((2, 2 * levels, half * rows // 2), F32),
            vmem((2, NZ, NY, per, half * rows // 2), F32),
            vmem((2, per, width), F32),
            vmem((2, per, width), F32),
            vmem((2, per, width), F32),
            vmem((2, per, width), F32),
            dma((9,)),
            dma((4,)),
            dma((4,)),
            dma,
            dma((NZ,)),
            dma((2,)),
            dma((2, NZ)),
            dma((2,)),
            dma((2,)),
            pltpu.SemaphoreType.REGULAR((2,)),
            pltpu.SemaphoreType.REGULAR,
        ],
        compiler_params=pltpu.CompilerParams(
            collective_id=0, has_side_effects=True, vmem_limit_bytes=56 * 2**20
        ),
        name="section",
    )(precursor, u_star, v_star, w_star, heights, vert, side, after, span)
    precursor_next, pressure = pl.pallas_call(
        finish,
        out_shape=(
            jax.ShapeDtypeStruct(precursor.shape, F32),
            jax.ShapeDtypeStruct((2, levels // groups * planes, width), F32),
        ),
        in_specs=[pl.BlockSpec(memory_space=pltpu.VMEM)] * 5 + [any_space],
        out_specs=(any_space,) * 2,
        scratch_shapes=[
            vmem((per, width), F32),
            vmem((half, per, width), F32),
            vmem((2, width // 128, levels // groups * planes, 128), F32),
            dma((2,)),
            dma((2 * width // 128,)),
        ],
        compiler_params=pltpu.CompilerParams(vmem_limit_bytes=32 * 2**20),
        name="finish",
    )(*(pltpu.with_memory_space_constraint(value, pltpu.VMEM) for value in held), inv)
    return precursor_next, pressure.reshape(2, levels // groups, planes, width)


def solution(mesh):
    placed = (
        P(None, "gx", "gy", None),
        P("gx", "gy", None),
        P("gx", "gy", None),
        P("gx", "gy", None),
        P("gx", "gy"),
    )
    return jax.shard_map(
        on_device,
        mesh=mesh,
        in_specs=placed,
        out_specs=(P(None, "gx", "gy", None), P(None, "gy", "gx", None)),
        check_vma=False,
    )
```
